32 devices in a mesh: dp: 8 (over z, x), shard: 4 (over y, core).
Axes of the slice: x: 2, y: 2, z: 4, core: 2. Of those that a mesh axis runs over, the one named last changes fastest.
Arguments:
- hidden_in: bfloat16 [8192, 1024], P(('dp', 'shard')), may hold values from -6 to 6
- memory: bfloat16 [16384, 1024], P(('dp', 'shard')), may hold values from -6 to 6
- dec_lengths: int32 [64], P(('dp', 'shard')), may hold values from 16 to 128, as said below
- mem_lengths: int32 [64], P(('dp', 'shard')), may hold values from 64 to 256, as said below
- cotangent: bfloat16 [8192, 1024], P(('dp', 'shard')), may hold values from -6 to 6
- self_project: bfloat16 [1024, 3072], P(('dp', 'shard')), may hold values from -0.1875 to 0.1875
- self_output: bfloat16 [1024, 1024], P(('dp', 'shard')), may hold values from -1.5 to 1.5
- cross_query: bfloat16 [1024, 1024], P(('dp', 'shard')), may hold values from -0.1875 to 0.1875
- cross_memory: bfloat16 [1024, 2048], P(('dp', 'shard')), may hold values from -0.1875 to 0.1875
- cross_output: bfloat16 [1024, 1024], P(('dp', 'shard')), may hold values from -1.5 to 1.5
- feed_in: bfloat16 [1024, 4096], P(('dp', 'shard')), may hold values from -0.1875 to 0.1875
- feed_out: bfloat16 [4096, 1024], P(('dp', 'shard')), may hold values from -0.1875 to 0.1875
- bias_rows: bfloat16 [7, 1024], P(None, ('dp', 'shard')), may hold values from -2 to 2
- feed_bias: bfloat16 [4096], P(('dp', 'shard')), may hold values from -2 to 2
- norm_gains: bfloat16 [3, 1024], P(None, ('dp', 'shard')), may hold values from 0.5 to 1.5
- norm_shifts: bfloat16 [3, 1024], P(None, ('dp', 'shard')), may hold values from -2 to 2
Outputs:
- block_out: bfloat16 [8192, 1024], P(('dp', 'shard'))
- grad_hidden: bfloat16 [8192, 1024], P(('dp', 'shard'))
- grad_memory: bfloat16 [16384, 1024], P(('dp', 'shard'))
- grad_self_project: float32 [1024, 3072], P(('dp', 'shard'))
- grad_self_output: float32 [1024, 1024], P(('dp', 'shard'))
- grad_cross_query: float32 [1024, 1024], P(('dp', 'shard'))
- grad_cross_memory: float32 [1024, 2048], P(('dp', 'shard'))
- grad_cross_output: float32 [1024, 1024], P(('dp', 'shard'))
- grad_feed_in: float32 [1024, 4096], P(('dp', 'shard'))
- grad_feed_out: float32 [4096, 1024], P(('dp', 'shard'))
- grad_bias_rows: float32 [7, 1024], P(None, ('dp', 'shard'))
- grad_feed_bias: float32 [4096], P(('dp', 'shard'))
- grad_norm_gains: float32 [3, 1024], P(None, ('dp', 'shard'))
- grad_norm_shifts: float32 [3, 1024], P(None, ('dp', 'shard'))
The draws below stay inside these ranges and needn't reach their ends.
Inputs may be any that keep to these rules, and one draw needn't show every extreme that they name: `dec_lengths`: at least one sequence has all 128 decoder tokens valid. `mem_lengths`: at least one sequence has all 256 memory tokens valid.
All inputs are finite; a program needn't handle non-finite values.
Results may differ from the reference program's by a relative error of at most 0.02.
Values may be sent and summed in bfloat16 or wider, within the bound.
A program may use at most 320 MiB of HBM per device.

```python
import math
import jax
import jax.numpy as jnp
from jax import lax

D = 1024
HEADS = 16
HEAD_DIM = 64
FF = 4096
DEC = 128
MEM = 256
SEQS = 64
TOKENS = 8192
MEMTOK = 16384


def draw_dec_lengths(key, part):
    key = jax.random.fold_in(key, 3)
    lengths = jax.random.randint(key, (SEQS,), max(1, DEC // 8), DEC + 1)
    spot = jax.random.randint(jax.random.fold_in(key, 11), (), 0, SEQS)
    return lengths.at[spot].set(DEC)


def draw_mem_lengths(key, part):
    key = jax.random.fold_in(key, 5)
    lengths = jax.random.randint(key, (SEQS,), max(1, MEM // 4), MEM + 1)
    spot = jax.random.randint(jax.random.fold_in(key, 13), (), 0, SEQS)
    return lengths.at[spot].set(MEM)


def shard_levels(own_key, extent, shards, smallest, top_value):
    loudness, own = 1.0, jax.random.fold_in(own_key, 6)
    for dim, parts in shards:
        heights = jnp.exp(jax.random.uniform(jax.random.fold_in(own, dim), (parts,), jnp.float32, smallest / len(shards), top_value / len(shards)))
        loudness = loudness * jnp.repeat(heights, extent[dim] // parts).reshape([-1 if axis == dim else 1 for axis in range(len(extent))])
    return loudness


def scatter_about(own_key, dims, scale, limit, split=(), held_as=jnp.bfloat16):
    level = shard_levels(own_key, dims, split, -0.22, 0.18) if split else 1.0
    entries = jax.random.normal(own_key, dims, jnp.float32) * scale * level
    return jnp.minimum(jnp.maximum(entries, -limit), limit).astype(held_as)


def setup_inputs(seed: int = 0) -> dict:
    streams_of = jax.random.split(jax.random.key(seed), 17)
    hidden_in = scatter_about(streams_of[0], (TOKENS, D), 1.0, 6.0, ((0, 32),))
    memory = scatter_about(streams_of[1], (MEMTOK, D), 1.0, 6.0, ((0, 32),))
    dec_lengths = draw_dec_lengths(jax.random.fold_in(streams_of[16], 71), 0)
    mem_lengths = draw_mem_lengths(jax.random.fold_in(streams_of[16], 71), 0)
    cotangent = scatter_about(streams_of[4], (TOKENS, D), 1.0, 6.0, ((0, 32),))
    self_project = scatter_about(streams_of[5], (D, 3 * D), D ** -0.5, 0.1875, ((0, 32),))
    self_output = scatter_about(streams_of[6], (D, D), (max(16, D * DEC // 8192)) ** -0.5, 1.5, ((0, 32),))
    cross_query = scatter_about(streams_of[7], (D, D), D ** -0.5, 0.1875, ((0, 32),))
    cross_memory = scatter_about(streams_of[8], (D, 2 * D), D ** -0.5, 0.1875, ((0, 32),))
    cross_output = scatter_about(streams_of[9], (D, D), (max(16, D * MEM // 16384)) ** -0.5, 1.5, ((0, 32),))
    feed_in = scatter_about(streams_of[10], (D, FF), D ** -0.5, 0.1875, ((0, 32),))
    feed_out = scatter_about(streams_of[11], (FF, D), (FF // 4) ** -0.5, 0.1875, ((0, 32),))
    bias_rows = scatter_about(streams_of[12], (7, D), 0.3, 2.0, ((1, 32),))
    feed_bias = scatter_about(streams_of[13], (FF,), 0.3, 2.0, ((0, 32),))
    norm_gains = jnp.clip(1.0 + 0.1 * jax.random.normal(streams_of[14], (3, D), jnp.float32), 0.5, 1.5).astype(jnp.bfloat16)
    norm_shifts = scatter_about(streams_of[15], (3, D), 0.3, 2.0, ((1, 32),))
    return {"hidden_in": hidden_in, "memory": memory, "dec_lengths": dec_lengths, "mem_lengths": mem_lengths, "cotangent": cotangent, "self_project": self_project, "self_output": self_output, "cross_query": cross_query, "cross_memory": cross_memory, "cross_output": cross_output, "feed_in": feed_in, "feed_out": feed_out, "bias_rows": bias_rows, "feed_bias": feed_bias, "norm_gains": norm_gains, "norm_shifts": norm_shifts}


@jax.custom_vjp
def low(v):
    return lax.optimization_barrier(v.astype(jnp.bfloat16)).astype(jnp.float32)

@jax.custom_vjp
def low_back(v):
    return v

def low_keep(v):
    return (low(v), None)

def low_pass(kept, grad):
    return (grad,)

def back_keep(v):
    return (v, None)

def back_low(kept, grad):
    return (low(grad),)
low.defvjp(low_keep, low_pass)
low_back.defvjp(back_keep, back_low)
highest = lax.Precision.HIGHEST
alpha_res = 300.0 ** 0.25
epsilon = 1e-05
gelu_coef = math.sqrt(2.0 / math.pi)

def gelu_tanh(value):
    inner = gelu_coef * (value + 0.044715 * value * value * value)
    return 0.5 * value * (1.0 + jnp.tanh(inner))

def matmul(rows_mat, weight):
    return jnp.einsum('bti,ij->btj', rows_mat, weight, precision=highest)

def rounded(value):
    return low(low_back(value))

def normalize(resid, gain, shift):
    center = resid - lax.optimization_barrier(jnp.mean(resid, -1, keepdims=True))
    inv_dev = lax.rsqrt(lax.optimization_barrier(jnp.mean(center * center, -1, keepdims=True)) + jnp.asarray(epsilon, resid.dtype))
    return center * inv_dev * gain + shift

def attend(queries, key_rows, value_rows, allowed):
    batch, query_len, _ = queries.shape
    key_len = key_rows.shape[1]
    query_heads = queries.reshape(batch, query_len, HEADS, HEAD_DIM)
    key_heads = key_rows.reshape(batch, key_len, HEADS, HEAD_DIM)
    value_heads = value_rows.reshape(batch, key_len, HEADS, HEAD_DIM)
    raw = jnp.einsum('bqhe,bkhe->bhqk', query_heads, key_heads, precision=highest)
    scale = jnp.asarray(HEAD_DIM ** (-0.5), raw.dtype)
    floor_value = jnp.asarray(-1000000000.0, raw.dtype)
    scores = jnp.where(allowed[:, None], low_back(raw) * scale, floor_value)
    top_score = lax.optimization_barrier(jnp.max(scores, -1, keepdims=True))
    expo = jnp.exp(scores - top_score)
    probabilities = low(expo / lax.optimization_barrier(jnp.sum(expo, -1, keepdims=True)))
    mixed = jnp.einsum('bhqk,bkhe->bqhe', probabilities, value_heads, precision=highest)
    return mixed.reshape(batch, query_len, D)

def forward(params, hidden, memory, dec_len, mem_len):
    self_project, self_output, cross_query, cross_memory, cross_output, feed_in, feed_out, bias_rows, feed_bias, norm_gains, norm_shifts = params
    alpha = jnp.asarray(alpha_res, hidden.dtype)
    row_ids = jnp.arange(DEC, dtype=jnp.int32)
    mem_ids = jnp.arange(MEM, dtype=jnp.int32)
    dec_len = dec_len.astype(jnp.int32)
    mem_len = mem_len.astype(jnp.int32)
    valid_rows = row_ids[None, :] < dec_len[:, None]
    causal = (row_ids[None, None, :] <= row_ids[None, :, None]) & valid_rows[:, None, :]
    mem_seen = jnp.broadcast_to((mem_ids[None, :] < mem_len[:, None])[:, None, :], (hidden.shape[0], DEC, MEM))
    projected = matmul(hidden, self_project)
    queries = rounded(projected[..., :D] + bias_rows[0])
    key_rows = rounded(projected[..., D:2 * D])
    value_rows = rounded(projected[..., 2 * D:] + bias_rows[1])
    mixed = rounded(attend(queries, key_rows, value_rows, causal))
    branch = low_back(matmul(mixed, self_output) + bias_rows[2])
    first = rounded(normalize(alpha * hidden + branch, norm_gains[0], norm_shifts[0]))
    cross_q = rounded(matmul(first, cross_query) + bias_rows[3])
    mem_proj = matmul(memory, cross_memory)
    cross_k = rounded(mem_proj[..., :D])
    cross_v = rounded(mem_proj[..., D:] + bias_rows[4])
    mixed_two = rounded(attend(cross_q, cross_k, cross_v, mem_seen))
    branch_two = low_back(matmul(mixed_two, cross_output) + bias_rows[5])
    second = rounded(normalize(alpha * first + branch_two, norm_gains[1], norm_shifts[1]))
    pre_act = low_back(matmul(second, feed_in) + feed_bias)
    active = low(gelu_tanh(pre_act))
    branch_three = low_back(matmul(active, feed_out) + bias_rows[6])
    normed = normalize(alpha * second + branch_three, norm_gains[2], norm_shifts[2])
    return jnp.where(valid_rows[..., None], normed, jnp.zeros_like(normed))

def reference(hidden_in, memory, dec_lengths, mem_lengths, cotangent, self_project, self_output, cross_query, cross_memory, cross_output, feed_in, feed_out, bias_rows, feed_bias, norm_gains, norm_shifts):
    params = tuple((item.astype(jnp.float32) for item in (self_project, self_output, cross_query, cross_memory, cross_output, feed_in, feed_out, bias_rows, feed_bias, norm_gains, norm_shifts)))
    float_type = params[0].dtype
    group = math.gcd(SEQS, max(1, 4096 // DEC))
    count = SEQS // group
    hidden_groups = hidden_in.astype(float_type).reshape(count, group, DEC, D)
    memory_groups = memory.astype(float_type).reshape(count, group, MEM, D)
    cot_groups = cotangent.astype(float_type).reshape(count, group, DEC, D)
    dec_groups = dec_lengths.astype(jnp.int32).reshape(count, group)
    mem_groups = mem_lengths.astype(jnp.int32).reshape(count, group)

    def step(totals, items):
        hidden, mem_rows, dec_len, mem_len, cot_rows = items
        result, pull = jax.vjp(lambda par, hid, mem: forward(par, hid, mem, dec_len, mem_len), params, hidden, mem_rows)
        grad_params, grad_hid, grad_mem = pull(cot_rows.astype(result.dtype))
        totals = jax.tree.map(lambda earlier, later: earlier + later.astype(earlier.dtype), totals, grad_params)
        return (totals, (result.astype(float_type), grad_hid.astype(float_type), grad_mem.astype(float_type)))
    zeros = tuple((jnp.zeros(item.shape, float_type) for item in params))
    totals, (outputs, grad_hidden, grad_memory) = lax.scan(step, zeros, (hidden_groups, memory_groups, dec_groups, mem_groups, cot_groups))
    factor = jnp.asarray(float(TOKENS) ** (-0.5), float_type)
    totals = tuple((item * factor for item in totals))
    return (outputs.reshape(TOKENS, D).astype(jnp.bfloat16), grad_hidden.reshape(TOKENS, D).astype(jnp.bfloat16), grad_memory.reshape(MEMTOK, D).astype(jnp.bfloat16), totals[0], totals[1], totals[2], totals[3], totals[4], totals[5], totals[6], totals[7], totals[8], totals[9], totals[10])
```

```python
import functools
import math

import jax
import jax.numpy as jnp
from jax import lax
from jax.experimental import pallas as pl
from jax.experimental.pallas import tpu as pltpu
from jax.sharding import PartitionSpec as P

D = 1024
HEADS = 16
HEAD_DIM = 64
DEC = 128
MEM = 256
AXES = ("dp", "shard")
MESH_ID = pl.DeviceIdType.MESH
BF16 = jnp.bfloat16
F32 = jnp.float32

alpha_res = 300.0**0.25
epsilon = 1e-05
gelu_coef = math.sqrt(2.0 / math.pi)

SIZES = {"z": 4, "x": 2, "y": 2}
SLOT = {"x": 0, "y": 1, "s": 2, "z": 2}


def my_place():
    dp, shard = lax.axis_index("dp"), lax.axis_index("shard")
    return {
        "z": lax.div(dp, 2),
        "x": lax.rem(dp, 2),
        "y": lax.div(shard, 2),
        "c": lax.rem(shard, 2),
    }


def device_of(place):
    return (place["z"] * 2 + place["x"], place["y"] * 2 + place["c"])


def partners(place, dim):
    if dim == "z":
        return [(2 + o, dict(place, z=lax.rem(place["z"] + o, 4))) for o in (1, 2, 3)]
    key = "c" if dim == "s" else dim
    return [(SLOT[dim], dict(place, **{key: 1 - place[key]}))]


def greet(place):
    barrier = pltpu.get_barrier_semaphore()
    others = [p for dim in "xysz" for _, p in partners(place, dim)]
    for other in others:
        pl.semaphore_signal(barrier, inc=1, device_id=device_of(other), device_id_type=MESH_ID)
    pl.semaphore_wait(barrier, len(others))


def block_at(place, whole):
    return tuple(pl.ds(0, SIZES.get(d, 2)) if d in whole else place[d] for d in ("z", "x", "y", "c"))


class Gather:
    def __init__(self, place, own, full, start, width, order, number, send_sem, recv_sem):
        self.place, self.own, self.full, self.order, self.number = place, own, full, order, number
        self.columns = pl.ds(start, width)
        self.send_sem, self.recv_sem = send_sem, recv_sem
        self.sent = []
        self.waiting = []

    def send(self, source, index, dim):
        target = self.full.at[(*index, slice(None), self.columns)]
        self.waiting = []
        for slot, other in partners(self.place, dim):
            copy = pltpu.make_async_remote_copy(
                src_ref=source,
                dst_ref=target,
                send_sem=self.send_sem.at[self.number, slot],
                recv_sem=self.recv_sem.at[self.number, slot],
                device_id=device_of(other),
                device_id_type=MESH_ID,
            )
            copy.start()
            self.waiting.append(copy)
            self.sent.append(copy)

    def arrive(self):
        for copy in self.waiting:
            copy.wait_recv()

    def stage(self, number):
        if number > 0:
            self.arrive()
        if number == 0:
            self.send(self.own.at[:, self.columns], block_at(self.place, ""), self.order[0])
        elif number < 3:
            index = block_at(self.place, self.order[:number])
            self.send(self.full.at[(*index, slice(None), self.columns)], index, self.order[number])
        elif number == 3:
            index = block_at(self.place, "zxy")
            self.send(self.full.at[(*index, slice(None), self.columns)], index, "s")

    def drain(self):
        for copy in self.sent:
            copy.wait_send()


def schedule(count, stages, lag):
    for step in range(count + (stages - 1) * lag):
        for stage in reversed(range(stages)):
            if 0 <= step - stage * lag < count:
                yield step - stage * lag, stage


def gather_plan(blocks, size):
    plan = []
    for unit, (rows, columns) in enumerate(blocks):
        width = min(columns, size // rows)
        for start in range(0, columns, width):
            plan.append((unit, start, width, GATHER_ORDERS[len(plan) % len(GATHER_ORDERS)]))
    return plan


LAG = 3
WIDTH = 512
SLOTS = 3
GATHER_ORDERS = ("xzy", "zyx", "zxy", "yzx", "zyx", "zxy")


def gather_kernel(plan, units, *refs):
    own, full = refs[:units], refs[units : 2 * units]
    send_sem, recv_sem, own_sem = refs[2 * units :]
    place = my_place()
    greet(place)
    here = []
    for unit in range(units):
        copy = pltpu.make_async_copy(own[unit], full[unit].at[block_at(place, "")], own_sem.at[unit])
        copy.start()
        here.append(copy)
    chunks = [
        Gather(place, own[unit], full[unit], start, width, order, number, send_sem, recv_sem)
        for number, (unit, start, width, order) in enumerate(plan)
    ]
    for copy in here:
        copy.wait()
    for number, stage in schedule(len(chunks), 5, LAG):
        chunks[number].stage(stage)
    for chunk in chunks:
        chunk.drain()


def gather_all(owned):
    units = len(owned)
    plan = gather_plan([a.shape for a in owned], 32 * WIDTH)
    any_spec = pl.BlockSpec(memory_space=pl.ANY)
    return pl.pallas_call(
        functools.partial(gather_kernel, plan, units),
        out_shape=[jax.ShapeDtypeStruct((4, 2, 2, 2, *a.shape), a.dtype) for a in owned],
        in_specs=[any_spec] * units,
        out_specs=[any_spec] * units,
        scratch_shapes=[
            pltpu.SemaphoreType.DMA((len(plan), 6)),
            pltpu.SemaphoreType.DMA((len(plan), 6)),
            pltpu.SemaphoreType.DMA((units,)),
        ],
        compiler_params=pltpu.CompilerParams(collective_id=0, has_side_effects=True),
        name="gather_parameters",
    )(*owned)


SCATTER_ORDERS = ("yzx", "xyz", "yxz", "xzy", "xyz", "yxz")


def rings_of(order):
    keys = [("s", "zxy")]
    left = "zxy"
    for dim in order:
        left = left.replace(dim, "")
        keys.append((dim, left))
    return keys


def ring_shape(key, width):
    dim, left = key
    return (SLOTS, 3 if dim == "z" else 1, *[SIZES[d] for d in left], 32, width)


class Rings:
    def __init__(self, place, keys, buffers, credit, plan):
        self.place, self.credit = place, credit
        self.number = {key: k for k, key in enumerate(keys)}
        self.buffer = dict(zip(keys, buffers))
        self.uses = {key: 0 for key in keys}
        for _, _, _, _, _, order in plan:
            for key in rings_of(order):
                self.uses[key] += 1
        self.turn = {key: 0 for key in keys}

    def take(self, key):
        turn = self.turn[key]
        self.turn[key] += 1
        if turn >= SLOTS:
            for slot, _ in partners(self.place, key[0]):
                pl.semaphore_wait(self.credit.at[self.number[key], slot], 1)
        return turn

    def give(self, key, turn):
        if turn + SLOTS >= self.uses[key]:
            return
        for slot, other in partners(self.place, key[0]):
            if key[0] == "z":
                other = dict(self.place, z=lax.rem(self.place["z"] + 6 - slot, 4))
            pl.semaphore_signal(
                self.credit.at[self.number[key], slot], inc=1, device_id=device_of(other), device_id_type=MESH_ID
            )


class Scatter:
    def __init__(self, place, rings, grads, out, scale, piece, number, send_sem, recv_sem):
        _, row, rows, start, width, self.order = piece
        self.place, self.rings, self.grads, self.out, self.scale, self.number = place, rings, grads, out, scale, number
        self.part = (pl.ds(row, rows), pl.ds(start, width))
        self.corner = (pl.ds(0, rows), pl.ds(0, width))
        self.keys = rings_of(self.order)
        self.send_sem, self.recv_sem = send_sem, recv_sem
        self.sent = []

    def send(self, stage):
        key = self.keys[stage]
        dim, left = key
        self.turn = self.rings.take(key)
        buffer = self.rings.buffer[key]
        self.waiting = []
        for k, (slot, other) in enumerate(partners(self.place, dim)):
            copy = pltpu.make_async_remote_copy(
                src_ref=self.grads.at[(*block_at(other, left), *self.part)],
                dst_ref=buffer.at[(self.turn % SLOTS, k, *[slice(None)] * len(left), *self.corner)],
                send_sem=self.send_sem.at[self.number, slot],
                recv_sem=self.recv_sem.at[self.number, slot],
                device_id=device_of(other),
                device_id_type=MESH_ID,
            )
            copy.start()
            self.waiting.append(copy)
            self.sent.append(copy)

    def add(self, stage):
        key = self.keys[stage]
        dim, left = key
        for copy in self.waiting:
            copy.wait_recv()
        buffer = self.rings.buffer[key]
        slot = self.turn % SLOTS

        def total(inner, own):
            value = self.grads[(*own, *self.part)].astype(F32)
            for k in range(3 if dim == "z" else 1):
                value += buffer[(slot, k, *inner, *self.corner)].astype(F32)
            return value

        own = block_at(self.place, left)
        if not left:
            self.out[self.part] = total((), own) * self.scale
        elif len(left) == 1:
            inner = (slice(None),)
            self.grads[(*own, *self.part)] = total(inner, own).astype(BF16)
        else:
            first = left[0]

            def body(i, _):
                here = dict(self.place, **{first: i})
                index = block_at(here, left[1:])
                inner = (i, *[slice(None)] * (len(left) - 1))
                self.grads[(*index, *self.part)] = total(inner, index).astype(BF16)
                return 0

            lax.fori_loop(0, SIZES[first], body, 0)
        self.rings.give(key, self.turn)

    def stage(self, number):
        if number > 0:
            self.add(number - 1)
        if number < 4:
            self.send(number)

    def drain(self):
        for copy in self.sent:
            copy.wait_send()


def scatter_plan(blocks, width):
    plan = []
    for unit, (rows, columns) in enumerate(blocks):
        for row in range(0, rows, 32):
            for start in range(0, columns, width):
                order = SCATTER_ORDERS[len(plan) % len(SCATTER_ORDERS)]
                plan.append((unit, row, min(rows, 32), start, min(columns, width), order))
    return plan


def ring_keys():
    return sorted({key for order in SCATTER_ORDERS for key in rings_of(order)})


def scatter_kernel(plan, scale, units, *refs):
    grads, outs, held = refs[:units], refs[units : 2 * units], refs[2 * units : 3 * units]
    keys = ring_keys()
    buffers = refs[3 * units : 3 * units + len(keys)]
    send_sem, recv_sem, load_sem, credit = refs[3 * units + len(keys) :]
    place = my_place()
    greet(place)
    rings = Rings(place, keys, buffers, credit, plan)
    loads, chunks = [], []
    everywhere = (slice(None),) * 4
    for number, piece in enumerate(plan):
        unit = piece[0]
        chunk = Scatter(place, rings, held[unit], outs[unit], scale, piece, number, send_sem, recv_sem)
        where = (*everywhere, *chunk.part)
        load = pltpu.make_async_copy(grads[unit].at[where], held[unit].at[where], load_sem.at[number])
        load.start()
        loads.append(load)
        chunks.append(chunk)

    for number, stage in schedule(len(chunks), 5, LAG):
        if stage == 0:
            loads[number].wait()
        chunks[number].stage(stage)
    for chunk in chunks:
        chunk.drain()


def scatter_all(grads, scale):
    units = len(grads)
    plan = scatter_plan([a.shape[4:] for a in grads], WIDTH)
    any_spec = pl.BlockSpec(memory_space=pl.ANY)
    vmem = pl.BlockSpec(memory_space=pltpu.VMEM)
    keys = ring_keys()
    return pl.pallas_call(
        functools.partial(scatter_kernel, plan, scale, units),
        out_shape=[jax.ShapeDtypeStruct(a.shape[4:], F32) for a in grads],
        in_specs=[any_spec] * units,
        out_specs=[vmem] * units,
        scratch_shapes=[pltpu.VMEM(a.shape, BF16) for a in grads]
        + [pltpu.VMEM(ring_shape(key, WIDTH), BF16) for key in keys]
        + [
            pltpu.SemaphoreType.DMA((len(plan), 6)),
            pltpu.SemaphoreType.DMA((len(plan), 6)),
            pltpu.SemaphoreType.DMA((len(plan),)),
            pltpu.SemaphoreType.REGULAR((len(keys), 6)),
        ],
        compiler_params=pltpu.CompilerParams(collective_id=1, has_side_effects=True, vmem_limit_bytes=58 * 2**20),
        name="scatter_gradients",
    )(*grads)


def gelu_tanh(value):
    inner = gelu_coef * (value + 0.044715 * value * value * value)
    return 0.5 * value * (1.0 + jnp.tanh(inner))


def gelu_slope(value):
    inner = gelu_coef * (value + 0.044715 * value * value * value)
    tangent = jnp.tanh(inner)
    return 0.5 * (1.0 + tangent) + 0.5 * value * (1.0 - tangent * tangent) * gelu_coef * (
        1.0 + 3.0 * 0.044715 * value * value
    )


def product(rows_mat, weight):
    return jnp.dot(rows_mat, weight, preferred_element_type=F32)


def times_trans(rows_mat, weight):
    return jnp.einsum("tj,ij->ti", rows_mat, weight, preferred_element_type=F32)


def outer_sum(left_rows, right_rows):
    return jnp.einsum("ti,tj->ij", left_rows, right_rows, preferred_element_type=F32)


def column_total(rows_mat):
    return jnp.sum(rows_mat.astype(F32), 0)


def layer_norm(resid, gain, shift):
    center = resid - jnp.mean(resid, -1, keepdims=True)
    inv_dev = lax.rsqrt(jnp.mean(center * center, -1, keepdims=True) + epsilon)
    scaled = center * inv_dev
    return (scaled * gain + shift, scaled, inv_dev)


def norm_back(grad_out, scaled, inv_dev, gain):
    grad_scaled = grad_out * gain
    grad_resid = inv_dev * (
        grad_scaled
        - jnp.mean(grad_scaled, -1, keepdims=True)
        - scaled * jnp.mean(grad_scaled * scaled, -1, keepdims=True)
    )
    return (grad_resid, jnp.sum(grad_out * scaled, 0), jnp.sum(grad_out, 0))


def split_heads(matrix, length):
    return matrix.reshape(-1, length, HEADS, HEAD_DIM)


def merge_heads(tensor):
    return tensor.reshape(-1, D)


def scores_of(query_rows, key_rows, allowed):
    keys = allowed.shape[-1]
    raw = jnp.einsum(
        "sqhe,skhe->shqk",
        split_heads(query_rows, DEC),
        split_heads(key_rows, keys),
        preferred_element_type=F32,
    )
    return jnp.where(allowed[:, None], raw * HEAD_DIM ** (-0.5), -1000000000.0)


def attend(query_rows, key_rows, value_rows, allowed):
    scores = scores_of(query_rows, key_rows, allowed)
    top_score = jnp.max(scores, -1, keepdims=True)
    log_total = top_score + jnp.log(jnp.sum(jnp.exp(scores - top_score), -1, keepdims=True))
    probabilities = jnp.exp(scores - log_total).astype(BF16)
    mixed = jnp.einsum(
        "shqk,skhe->sqhe",
        probabilities,
        split_heads(value_rows, allowed.shape[-1]),
        preferred_element_type=F32,
    )
    return (merge_heads(mixed).astype(BF16), log_total)


def attend_back(query_rows, key_rows, value_rows, allowed, log_total, grad_mixed):
    keys = allowed.shape[-1]
    probabilities = jnp.exp(scores_of(query_rows, key_rows, allowed) - log_total)
    grad_heads = split_heads(grad_mixed, DEC)
    grad_value = jnp.einsum(
        "shqk,sqhe->skhe", probabilities.astype(BF16), grad_heads, preferred_element_type=F32
    )
    grad_probs = jnp.einsum(
        "sqhe,skhe->shqk", grad_heads, split_heads(value_rows, keys), preferred_element_type=F32
    )
    grad_scores = probabilities * (
        grad_probs - jnp.sum(probabilities * grad_probs, -1, keepdims=True)
    )
    grad_raw = (grad_scores * HEAD_DIM ** (-0.5)).astype(BF16)
    grad_query = jnp.einsum(
        "shqk,skhe->sqhe", grad_raw, split_heads(key_rows, keys), preferred_element_type=F32
    )
    grad_key = jnp.einsum(
        "shqk,sqhe->skhe", grad_raw, split_heads(query_rows, DEC), preferred_element_type=F32
    )
    return (
        merge_heads(grad_query).astype(BF16),
        merge_heads(grad_key).astype(BF16),
        merge_heads(grad_value).astype(BF16),
    )


def masks_for(dec_lengths, mem_lengths):
    row_ids = jnp.arange(DEC)
    inside = row_ids[None, :] < dec_lengths[:, None]
    valid_rows = inside.reshape(-1, 1)
    causal = (row_ids[None, None, :] <= row_ids[None, :, None]) & inside[:, None, :]
    mem_seen = (jnp.arange(MEM)[None, :] < mem_lengths[:, None])[:, None, :]
    mem_seen = jnp.broadcast_to(mem_seen, (mem_lengths.shape[0], DEC, MEM))
    return (valid_rows, causal, mem_seen)


def run_forward(weights, hidden, mem_rows, dec_lengths, mem_lengths):
    (
        self_project,
        self_output,
        cross_query,
        cross_memory,
        cross_output,
        feed_in,
        feed_out,
        bias_rows,
        feed_bias,
        norm_gains,
        norm_shifts,
    ) = weights
    bias_full = bias_rows.astype(F32)
    gain_full = norm_gains.astype(F32)
    shift_full = norm_shifts.astype(F32)
    valid_rows, causal, mem_seen = masks_for(dec_lengths, mem_lengths)
    projected = product(hidden, self_project)
    query_rows = (projected[:, :D] + bias_full[0]).astype(BF16)
    key_rows = projected[:, D : 2 * D].astype(BF16)
    value_rows = (projected[:, 2 * D :] + bias_full[1]).astype(BF16)
    mixed, log_one = attend(query_rows, key_rows, value_rows, causal)
    resid_one = alpha_res * hidden.astype(F32) + product(mixed, self_output) + bias_full[2]
    first, scaled_one, inv_one = layer_norm(resid_one, gain_full[0], shift_full[0])
    first = first.astype(BF16)
    cross_q = (product(first, cross_query) + bias_full[3]).astype(BF16)
    mem_proj = product(mem_rows, cross_memory)
    cross_k = mem_proj[:, :D].astype(BF16)
    cross_v = (mem_proj[:, D:] + bias_full[4]).astype(BF16)
    mixed_two, log_two = attend(cross_q, cross_k, cross_v, mem_seen)
    resid_two = (
        alpha_res * first.astype(F32) + product(mixed_two, cross_output) + bias_full[5]
    )
    second, scaled_two, inv_two = layer_norm(resid_two, gain_full[1], shift_full[1])
    second = second.astype(BF16)
    pre_act = product(second, feed_in) + feed_bias.astype(F32)
    active = gelu_tanh(pre_act).astype(BF16)
    resid_three = alpha_res * second.astype(F32) + product(active, feed_out) + bias_full[6]
    normed, scaled_three, inv_three = layer_norm(resid_three, gain_full[2], shift_full[2])
    block_out = jnp.where(valid_rows, normed, 0.0).astype(BF16)
    saved = (
        query_rows,
        key_rows,
        value_rows,
        log_one,
        mixed,
        scaled_one,
        inv_one,
        first,
        cross_q,
        cross_k,
        cross_v,
        log_two,
        mixed_two,
        scaled_two,
        inv_two,
        second,
        pre_act,
        active,
        scaled_three,
        inv_three,
    )
    return (saved, block_out)


def run_backward(weights, saved, hidden, mem_rows, cot_rows, dec_lengths, mem_lengths):
    (
        self_project,
        self_output,
        cross_query,
        cross_memory,
        cross_output,
        feed_in,
        feed_out,
        bias_rows,
        feed_bias,
        norm_gains,
        norm_shifts,
    ) = weights
    (
        query_rows,
        key_rows,
        value_rows,
        log_one,
        mixed,
        scaled_one,
        inv_one,
        first,
        cross_q,
        cross_k,
        cross_v,
        log_two,
        mixed_two,
        scaled_two,
        inv_two,
        second,
        pre_act,
        active,
        scaled_three,
        inv_three,
    ) = saved
    gain_full = norm_gains.astype(F32)
    valid_rows, causal, mem_seen = masks_for(dec_lengths, mem_lengths)
    grad_top = jnp.where(valid_rows, cot_rows.astype(F32), 0.0)
    grad_three, gain_three, shift_three = norm_back(grad_top, scaled_three, inv_three, gain_full[2])
    branch_three = grad_three.astype(BF16)
    grad_feed_out = outer_sum(active, branch_three)
    grad_pre = (times_trans(branch_three, feed_out) * gelu_slope(pre_act)).astype(BF16)
    grad_feed_in = outer_sum(second, grad_pre)
    grad_second = (alpha_res * grad_three + times_trans(grad_pre, feed_in)).astype(BF16)
    grad_two, gain_two, shift_two = norm_back(
        grad_second.astype(F32), scaled_two, inv_two, gain_full[1]
    )
    branch_two = grad_two.astype(BF16)
    grad_cross_output = outer_sum(mixed_two, branch_two)
    grad_mixed_two = times_trans(branch_two, cross_output).astype(BF16)
    grad_cq, grad_ck, grad_cv = attend_back(
        cross_q, cross_k, cross_v, mem_seen, log_two, grad_mixed_two
    )
    grad_mem_proj = jnp.concatenate([grad_ck, grad_cv], 1)
    grad_cross_memory = outer_sum(mem_rows, grad_mem_proj)
    grad_mem_rows = times_trans(grad_mem_proj, cross_memory).astype(BF16)
    grad_cross_query = outer_sum(first, grad_cq)
    grad_first = (alpha_res * grad_two + times_trans(grad_cq, cross_query)).astype(BF16)
    grad_one, gain_one, shift_one = norm_back(
        grad_first.astype(F32), scaled_one, inv_one, gain_full[0]
    )
    branch_one = grad_one.astype(BF16)
    grad_self_output = outer_sum(mixed, branch_one)
    grad_mixed = times_trans(branch_one, self_output).astype(BF16)
    grad_q, grad_k, grad_v = attend_back(
        query_rows, key_rows, value_rows, causal, log_one, grad_mixed
    )
    grad_projected = jnp.concatenate([grad_q, grad_k, grad_v], 1)
    grad_self_project = outer_sum(hidden, grad_projected)
    grad_hidden = (alpha_res * grad_one + times_trans(grad_projected, self_project)).astype(
        BF16
    )
    grad_bias_rows = jnp.stack(
        [
            column_total(grad_q),
            column_total(grad_v),
            column_total(branch_one),
            column_total(grad_cq),
            column_total(grad_cv),
            column_total(branch_two),
            column_total(branch_three),
        ]
    )
    grads = (
        grad_self_project,
        grad_self_output,
        grad_cross_query,
        grad_cross_memory,
        grad_cross_output,
        grad_feed_in,
        grad_feed_out,
        grad_bias_rows,
        column_total(grad_pre),
        jnp.stack([gain_one, gain_two, gain_three]),
        jnp.stack([shift_one, shift_two, shift_three]),
    )
    return (grads, grad_hidden, grad_mem_rows)


SMALL = 13


def pack_small(bias_rows, feed_bias, norm_gains, norm_shifts):
    rows = jnp.concatenate([bias_rows, norm_gains, norm_shifts], 0)
    span = rows.shape[1]
    lane = lax.broadcasted_iota(jnp.int32, (SMALL, 128), 1) // span
    rows = jnp.where(lane == lax.axis_index("shard"), jnp.tile(rows, (1, 128 // span)), 0)
    rest = jnp.zeros((2, 128), BF16)
    return jnp.concatenate([rows, feed_bias[None], rest], 0)


def unpack_small(blocks):
    rows = blocks[:, :SMALL].reshape(-1, 4, SMALL, 128).astype(F32).sum(1).astype(BF16)
    rows = rows.transpose(1, 0, 2).reshape(SMALL, D)
    return rows[:7], blocks[:, SMALL].reshape(-1), rows[7:10], rows[10:]


def pack_small_grads(grad_bias_rows, grad_feed_bias, grad_gains, grad_shifts):
    rows = jnp.concatenate([grad_bias_rows, grad_gains, grad_shifts], 0)
    rows = rows.reshape(SMALL, 8, 1, 128).transpose(1, 2, 0, 3)
    rows = jnp.broadcast_to(rows, (8, 4, SMALL, 128)).reshape(32, SMALL, 128)
    feed = grad_feed_bias.reshape(32, 1, 128)
    return jnp.concatenate([rows, feed, jnp.zeros((32, 2, 128), F32)], 1).astype(BF16)


def unpack_small_grads(block):
    rows = lax.dynamic_slice_in_dim(block[:SMALL], lax.axis_index("shard") * 32, 32, 1)
    return rows[:7], block[SMALL], rows[7:10], rows[10:]


def gather_by_collectives(owned):
    axis = [0] * 7 + [1, 0, 1, 1]
    return tuple(lax.all_gather(a, AXES, axis=d, tiled=True) for a, d in zip(owned, axis))


def scatter_by_collectives(grads, factor):
    axis = [0] * 7 + [1, 0, 1, 1]
    return tuple(
        lax.psum_scatter(a * factor, AXES, scatter_dimension=d, tiled=True) for a, d in zip(grads, axis)
    )


def body(by_kernel, hidden_in, memory, dec_lengths, mem_lengths, cotangent, *owned):
    token_count = hidden_in.shape[0] * lax.axis_size(AXES)
    factor = float(token_count) ** (-0.5)
    if by_kernel:
        big = gather_all((pack_small(*owned[7:]), *owned[:7]))
        small = unpack_small(big[0].reshape(-1, 16, 128))
        weights = (*[a.reshape(-1, a.shape[-1]) for a in big[1:]], *small)
    else:
        weights = gather_by_collectives(owned)
    saved, block_out = run_forward(weights, hidden_in, memory, dec_lengths, mem_lengths)
    grads, grad_hidden, grad_memory = run_backward(
        weights, saved, hidden_in, memory, cotangent, dec_lengths, mem_lengths
    )
    if by_kernel:
        small = pack_small_grads(*grads[7:])
        packed = [a.astype(BF16).reshape(32, -1, a.shape[-1]) for a in grads[:7]]
        packed = [a.reshape(4, 2, 2, 2, *a.shape[1:]) for a in (small, *packed)]
        shares = scatter_all(packed, factor)
        totals = (*shares[1:], *unpack_small_grads(shares[0]))
    else:
        totals = scatter_by_collectives(grads, factor)
    return (block_out, grad_hidden, grad_memory, *totals)


def solution(mesh):
    rows, columns, vector = P(AXES, None), P(None, AXES), P(AXES)
    in_specs = (rows, rows, vector, vector, rows, *[rows] * 7, columns, vector, columns, columns)
    out_specs = (rows, rows, rows, *[rows] * 7, columns, vector, columns, columns)
    by_kernel = mesh.shape["dp"] == 8 and mesh.shape["shard"] == 4
    return jax.shard_map(
        functools.partial(body, by_kernel), mesh=mesh, in_specs=in_specs, out_specs=out_specs, check_vma=False
    )
```

```python
import functools
import math

import jax
import jax.numpy as jnp
from jax import lax
from jax.experimental import pallas as pl
from jax.experimental.pallas import tpu as pltpu
from jax.sharding import PartitionSpec as P

D = 1024
HEADS = 16
HEAD_DIM = 64
DEC = 128
MEM = 256
AXES = ("dp", "shard")
MESH_ID = pl.DeviceIdType.MESH
BF16 = jnp.bfloat16
F32 = jnp.float32

alpha_res = 300.0**0.25
epsilon = 1e-05
gelu_coef = math.sqrt(2.0 / math.pi)

SIZES = {"z": 4, "x": 2, "y": 2}
SLOT = {"x": 0, "y": 1, "s": 2, "z": 2}


def my_place():
    dp, shard = lax.axis_index("dp"), lax.axis_index("shard")
    return {
        "z": lax.div(dp, 2),
        "x": lax.rem(dp, 2),
        "y": lax.div(shard, 2),
        "c": lax.rem(shard, 2),
    }


def device_of(place):
    return (place["z"] * 2 + place["x"], place["y"] * 2 + place["c"])


def partners(place, dim):
    if dim == "z":
        return [(2 + o, dict(place, z=lax.rem(place["z"] + o, 4))) for o in (1, 2, 3)]
    key = "c" if dim == "s" else dim
    return [(SLOT[dim], dict(place, **{key: 1 - place[key]}))]


def greet(place):
    barrier = pltpu.get_barrier_semaphore()
    others = [p for dim in "xysz" for _, p in partners(place, dim)]
    for other in others:
        pl.semaphore_signal(barrier, inc=1, device_id=device_of(other), device_id_type=MESH_ID)
    pl.semaphore_wait(barrier, len(others))


def block_at(place, whole):
    return tuple(pl.ds(0, SIZES.get(d, 2)) if d in whole else place[d] for d in ("z", "x", "y", "c"))


class Gather:
    def __init__(self, place, own, full, start, width, order, number, send_sem, recv_sem):
        self.place, self.own, self.full, self.order, self.number = place, own, full, order, number
        self.columns = pl.ds(start, width)
        self.send_sem, self.recv_sem = send_sem, recv_sem
        self.sent = []
        self.waiting = []

    def send(self, source, index, dim):
        target = self.full.at[(*index, slice(None), self.columns)]
        self.waiting = []
        for slot, other in partners(self.place, dim):
            copy = pltpu.make_async_remote_copy(
                src_ref=source,
                dst_ref=target,
                send_sem=self.send_sem.at[self.number, slot],
                recv_sem=self.recv_sem.at[self.number, slot],
                device_id=device_of(other),
                device_id_type=MESH_ID,
            )
            copy.start()
            self.waiting.append(copy)
            self.sent.append(copy)

    def arrive(self):
        for copy in self.waiting:
            copy.wait_recv()

    def stage(self, number):
        if number > 0:
            self.arrive()
        if number == 0:
            self.send(self.own.at[:, self.columns], block_at(self.place, ""), self.order[0])
        elif number < 3:
            index = block_at(self.place, self.order[:number])
            self.send(self.full.at[(*index, slice(None), self.columns)], index, self.order[number])
        elif number == 3:
            index = block_at(self.place, "zxy")
            self.send(self.full.at[(*index, slice(None), self.columns)], index, "s")

    def drain(self):
        for copy in self.sent:
            copy.wait_send()


def schedule(count, stages, lag):
    for step in range(count + (stages - 1) * lag):
        for stage in reversed(range(stages)):
            if 0 <= step - stage * lag < count:
                yield step - stage * lag, stage


def gather_plan(units, size):
    plan = []
    for unit in units:
        rows, columns = BLOCKS[unit]
        width = min(columns, size // rows)
        for start in range(0, columns, width):
            plan.append((unit, start, width, GATHER_ORDERS[len(plan) % len(GATHER_ORDERS)]))
    return plan


FF = 4096
LAG = 3
FORWARD_SHARE = 4.0
BACKWARD_SHARE = 3.0
VMEM_LIMIT = 62 * 2**20
WIDTH = 512
SLOTS = 3
GATHER_ORDERS = ("xzy", "zyx", "zxy", "yzx", "zyx", "zxy")


SCATTER_ORDERS = ("yzx", "xyz", "yxz", "xzy", "xyz", "yxz")


def rings_of(order):
    keys = [("s", "zxy")]
    left = "zxy"
    for dim in order:
        left = left.replace(dim, "")
        keys.append((dim, left))
    return keys


def ring_shape(key, width):
    dim, left = key
    return (SLOTS, 3 if dim == "z" else 1, *[SIZES[d] for d in left], 32, width)


class Rings:
    def __init__(self, place, keys, buffers, credit, plan):
        self.place, self.credit = place, credit
        self.number = {key: k for k, key in enumerate(keys)}
        self.buffer = dict(zip(keys, buffers))
        self.uses = {key: 0 for key in keys}
        for _, _, _, _, _, order in plan:
            for key in rings_of(order):
                self.uses[key] += 1
        self.turn = {key: 0 for key in keys}

    def take(self, key):
        turn = self.turn[key]
        self.turn[key] += 1
        if turn >= SLOTS:
            for slot, _ in partners(self.place, key[0]):
                pl.semaphore_wait(self.credit.at[self.number[key], slot], 1)
        return turn

    def give(self, key, turn):
        if turn + SLOTS >= self.uses[key]:
            return
        for slot, other in partners(self.place, key[0]):
            if key[0] == "z":
                other = dict(self.place, z=lax.rem(self.place["z"] + 6 - slot, 4))
            pl.semaphore_signal(
                self.credit.at[self.number[key], slot], inc=1, device_id=device_of(other), device_id_type=MESH_ID
            )


class Scatter:
    def __init__(self, place, rings, grads, out, scale, piece, number, send_sem, recv_sem):
        _, row, rows, start, width, self.order = piece
        self.place, self.rings, self.grads, self.out, self.scale, self.number = place, rings, grads, out, scale, number
        self.part = (pl.ds(row, rows), pl.ds(start, width))
        self.corner = (pl.ds(0, rows), pl.ds(0, width))
        self.keys = rings_of(self.order)
        self.send_sem, self.recv_sem = send_sem, recv_sem
        self.sent = []

    def send(self, stage):
        key = self.keys[stage]
        dim, left = key
        self.turn = self.rings.take(key)
        buffer = self.rings.buffer[key]
        self.waiting = []
        for k, (slot, other) in enumerate(partners(self.place, dim)):
            copy = pltpu.make_async_remote_copy(
                src_ref=self.grads.at[(*block_at(other, left), *self.part)],
                dst_ref=buffer.at[(self.turn % SLOTS, k, *[slice(None)] * len(left), *self.corner)],
                send_sem=self.send_sem.at[self.number, slot],
                recv_sem=self.recv_sem.at[self.number, slot],
                device_id=device_of(other),
                device_id_type=MESH_ID,
            )
            copy.start()
            self.waiting.append(copy)
            self.sent.append(copy)

    def add(self, stage):
        key = self.keys[stage]
        dim, left = key
        for copy in self.waiting:
            copy.wait_recv()
        buffer = self.rings.buffer[key]
        slot = self.turn % SLOTS

        def total(inner, own):
            value = self.grads[(*own, *self.part)].astype(F32)
            for k in range(3 if dim == "z" else 1):
                value += buffer[(slot, k, *inner, *self.corner)].astype(F32)
            return value

        own = block_at(self.place, left)
        if not left:
            self.out[self.part] = total((), own) * self.scale
        elif len(left) == 1:
            inner = (slice(None),)
            self.grads[(*own, *self.part)] = total(inner, own).astype(BF16)
        else:
            first = left[0]

            def body(i, _):
                here = dict(self.place, **{first: i})
                index = block_at(here, left[1:])
                inner = (i, *[slice(None)] * (len(left) - 1))
                self.grads[(*index, *self.part)] = total(inner, index).astype(BF16)
                return 0

            lax.fori_loop(0, SIZES[first], body, 0)
        self.rings.give(key, self.turn)

    def stage(self, number):
        if number > 0:
            self.add(number - 1)
        if number < 4:
            self.send(number)

    def drain(self):
        for copy in self.sent:
            copy.wait_send()


def scatter_plan(units, width):
    plan = []
    for unit in units:
        rows, columns = BLOCKS[unit]
        for row in range(0, rows, 32):
            for start in range(0, columns, width):
                order = SCATTER_ORDERS[len(plan) % len(SCATTER_ORDERS)]
                plan.append((unit, row, min(rows, 32), start, min(columns, width), order))
    return plan


def ring_keys():
    return sorted({key for order in SCATTER_ORDERS for key in rings_of(order)})


BLOCKS = ((16, 128), (32, 3 * D), (32, D), (32, D), (32, 2 * D), (32, D), (32, FF), (128, D))
GATHER_UNITS = (0, 1, 4, 2, 3, 5, 6, 7)
SCATTER_UNITS = (7, 6, 5, 4, 3, 2, 1, 0)
ROWS = 2 * DEC
KEYS = 2 * MEM


def dot(left, right):
    return jnp.dot(left, right, preferred_element_type=F32)


def dot_rows(left, right):
    return lax.dot_general(left, right, (((1,), (1,)), ((), ())), preferred_element_type=F32)


def dot_columns(left, right):
    return lax.dot_general(left, right, (((0,), (0,)), ((), ())), preferred_element_type=F32)


def flat(value):
    return value.reshape(-1, value.shape[-1])


def tile(index, size):
    return pl.ds(pl.multiple_of(index * size, size), size)


def loop(count, body):
    def step(i, carry):
        body(i)
        return carry

    lax.fori_loop(0, count, step, 0)


class Layer:
    def __init__(self, refs, dec_ref, mem_ref):
        self.dec_ref, self.mem_ref = dec_ref, mem_ref
        self.__dict__.update(refs)

    def unpack(self):
        small = self.weights[0]
        for group in range(8):
            block = small[group // 2, group % 2].astype(F32)
            self.vec[:, group * 128 : (group + 1) * 128] = block[0, 0] + block[0, 1] + block[1, 0] + block[1, 1]
            for k in range(4):
                first = (group * 4 + k) * 128
                self.feed[0:1, first : first + 128] = block[k // 2, k % 2, 13:14]
        self.sums[...] = jnp.zeros_like(self.sums)

    def row(self, number, columns=slice(None)):
        return self.vec[number : number + 1, columns]

    def project(self, start, width):
        out = dot(self.hidden[...], flat(self.weights[1][..., start : start + width]))
        if start < D:
            out += self.row(0, slice(start, start + width))
        elif start >= 2 * D:
            out += self.row(1, slice(start - 2 * D, start - 2 * D + width))
        self.qkv[:, start : start + width] = out.astype(BF16)

    def project_memory(self, start, width):
        weight = flat(self.weights[4][..., start : start + width])

        def half(i):
            out = dot(self.mem[tile(i, 256), :], weight)
            if start >= D:
                out += self.row(4, slice(start - D, start - D + width))
            self.kv2[tile(i, 256), start : start + width] = out.astype(BF16)

        loop(2, half)

    def output(self, unit, source, resid, bias, start, width):
        columns = slice(start, start + width)
        out = dot(source[...], flat(self.weights[unit][..., columns])) + self.row(bias, columns)
        self.acc[:, columns] = out + alpha_res * resid[:, columns].astype(F32)

    def query(self, start, width):
        columns = slice(start, start + width)
        out = dot(self.first[...], flat(self.weights[3][..., columns])) + self.row(3, columns)
        self.q2[:, columns] = out.astype(BF16)

    def feed_up(self, start, width):
        columns = slice(start, start + width)
        pre = dot(self.second[...], flat(self.weights[6][..., columns])) + self.feed[0:1, columns]
        square = pre * pre
        tangent = jnp.tanh(gelu_coef * pre * (1.0 + 0.044715 * square))
        self.act[:, columns] = (0.5 * pre * (1.0 + tangent)).astype(BF16)
        slope = 0.5 * (1.0 + tangent) + 0.5 * pre * (1.0 - tangent * tangent) * gelu_coef * (
            1.0 + 3.0 * 0.044715 * square
        )
        self.slope[:, columns] = slope.astype(BF16)

    def standard(self, rows):
        resid = self.acc[rows, :]
        center = resid - jnp.mean(resid, -1, keepdims=True)
        inv = lax.rsqrt(jnp.mean(center * center, -1, keepdims=True) + epsilon)
        return center * inv, inv

    def norm(self, number, out):
        def some(i):
            rows = tile(i, 64)
            scaled, inv = self.standard(rows)
            self.xhat[number, rows, :] = scaled.astype(BF16)
            self.inv[number, rows, :] = jnp.broadcast_to(inv, (64, 128))
            out[rows, :] = (scaled * self.row(7 + number) + self.row(10 + number)).astype(BF16)

        loop(4, some)

    def norm_grad(self, number, grad, scaled, inv, rows, b_ref):
        grad_scaled = grad * self.row(7 + number)
        resid = inv * (
            grad_scaled
            - jnp.mean(grad_scaled, -1, keepdims=True)
            - scaled * jnp.mean(grad_scaled * scaled, -1, keepdims=True)
        )
        branch = resid.astype(BF16)
        self.g[rows, :] = resid
        b_ref[rows, :] = branch
        bias = (2, 5, 6)[number]
        self.sums[7 + number : 8 + number, :] += jnp.sum(grad * scaled, 0, keepdims=True)
        self.sums[10 + number : 11 + number, :] += jnp.sum(grad, 0, keepdims=True)
        self.sums[bias : bias + 1, :] += jnp.sum(branch.astype(F32), 0, keepdims=True)

    def last_norm(self):
        def some(i):
            rows = tile(i, 64)
            scaled, inv = self.standard(rows)
            ids = lax.broadcasted_iota(jnp.int32, (64, 1), 0) + lax.rem(i, 2) * 64
            valid = ids < self.dec_ref[lax.div(i, 2)]
            grad = jnp.where(valid, self.do[rows, :].astype(F32), 0.0)
            out = scaled * self.row(9) + self.row(12)
            self.do[rows, :] = jnp.where(valid, out, 0.0).astype(BF16)
            self.norm_grad(2, grad, scaled, inv, rows, self.b_even)

        loop(4, some)

    def norm_back(self, number, b_ref):
        def some(i):
            rows = tile(i, 64)
            grad = self.acc[rows, :].astype(BF16).astype(F32)
            scaled = self.xhat[number, rows, :].astype(F32)
            self.norm_grad(number, grad, scaled, self.inv[number, rows, 0:1], rows, b_ref)

        loop(4, some)

    def stacked(self, value):
        low = lax.broadcasted_iota(jnp.int32, (DEC, 128), 1) < HEAD_DIM
        zero = jnp.zeros_like(value)
        return jnp.concatenate([jnp.where(low, value, zero), jnp.where(low, zero, value)], 0)

    def unstacked(self, value):
        low = lax.broadcasted_iota(jnp.int32, (DEC, 128), 1) < HEAD_DIM
        return jnp.where(low, value[:DEC], value[DEC:])

    def heads(self, cross, seq, pair):
        rows = tile(seq, DEC)
        if cross:
            keys, ref, first = tile(seq, MEM), self.kv2, 0
            q_at = (self.q2, rows, tile(pair, 128))
        else:
            keys, ref, first = rows, self.qkv, 8
            q_at = (self.qkv, rows, tile(pair, 128))
        k_at = (ref, keys, tile(first + pair, 128))
        v_at = (ref, keys, tile(first + 8 + pair, 128))
        return rows, q_at, k_at, v_at

    def weights_of(self, cross, seq, queries, key_rows):
        raw = dot_rows(queries, key_rows)
        column = lax.broadcasted_iota(jnp.int32, raw.shape, 1)
        if cross:
            allowed = column < self.mem_ref[seq]
        else:
            line = lax.rem(lax.broadcasted_iota(jnp.int32, raw.shape, 0), DEC)
            allowed = (column <= line) & (column < self.dec_ref[seq])
        scores = jnp.where(allowed, raw * HEAD_DIM ** (-0.5), -1000000000.0)
        expo = jnp.exp(scores - jnp.max(scores, -1, keepdims=True))
        return expo * (1.0 / jnp.sum(expo, -1, keepdims=True))

    def attend(self, cross, seq, pairs):
        out = self.mixed2 if cross else self.mixed

        def some(i):
            pair = i + pairs[0]
            rows, q_at, k_at, v_at = self.heads(cross, seq, pair)
            queries = self.stacked(q_at[0][q_at[1:]])
            probabilities = self.weights_of(cross, seq, queries, k_at[0][k_at[1:]])
            mixed = dot(probabilities.astype(BF16), v_at[0][v_at[1:]])
            out[rows, tile(pair, 128)] = self.unstacked(mixed).astype(BF16)

        loop(pairs[1] - pairs[0], some)

    def attend_back(self, cross, seq, pairs):
        def some(i):
            pair = i + pairs[0]
            rows, q_at, k_at, v_at = self.heads(cross, seq, pair)
            queries = self.stacked(q_at[0][q_at[1:]])
            key_rows, value_rows = k_at[0][k_at[1:]], v_at[0][v_at[1:]]
            grads = self.stacked(self.do[rows, tile(pair, 128)])
            probabilities = self.weights_of(cross, seq, queries, key_rows)
            grad_value = dot_columns(probabilities.astype(BF16), grads)
            grad_probs = dot_rows(grads, value_rows)
            mean = jnp.sum(probabilities * grad_probs, -1, keepdims=True)
            grad_raw = (probabilities * (grad_probs - mean) * HEAD_DIM ** (-0.5)).astype(BF16)
            grad_query = self.unstacked(dot(grad_raw, key_rows))
            grad_key = dot_columns(grad_raw, queries)
            q_at[0][q_at[1:]] = grad_query.astype(BF16)
            k_at[0][k_at[1:]] = grad_key.astype(BF16)
            v_at[0][v_at[1:]] = grad_value.astype(BF16)

        loop(pairs[1] - pairs[0], some)

    def feed_down_back(self, part):
        columns = slice(part * 512, part * 512 + 512)
        grad = dot_rows(self.b_even[...], flat(self.weights[7][part // 2, part % 2]))
        grad = (grad * self.slope[:, columns].astype(F32)).astype(BF16)
        self.slope[:, columns] = grad
        self.feed_sum[0:1, columns] = jnp.sum(grad.astype(F32), 0, keepdims=True)

    def back(self, unit, source, out, resid):
        def some(z):
            columns = tile(z, 256)
            value = dot_rows(source[...], flat(self.weights[unit][z]))
            if resid:
                value += alpha_res * self.g[:, columns]
            out[:, columns] = value.astype(out.dtype)

        loop(4, some)

    def total(self, number, source, columns):
        self.sums[number : number + 1, :] = jnp.sum(source[:, columns].astype(F32), 0, keepdims=True)

    def turn(self, source):
        for k in range(source.shape[0] // 256):
            for column in range(0, source.shape[1], 512):
                block = source[k * 256 : (k + 1) * 256, column : column + 512]
                first = k * source.shape[1] + column
                self.turned[first : first + 512, :] = block.T

    def turn_feed(self):
        for k in range(8):
            block = self.act[:, k * 512 : (k + 1) * 512].T
            self.turned_feed[k * 4 : (k + 1) * 4] = block.reshape(4, 128, 256)

    def outer(self, unit, source, piece):
        _, row, rows, start, width, _ = piece
        columns = slice(start, start + width)

        def some(z):
            if unit == 7:
                left = flat(self.turned_feed[tile(z, 8), row : row + rows, :])
                value = dot(left, source[:, columns])
            else:
                value = dot(self.turned[tile(z, 256), :], source[0:256, columns])
                if unit == 4:
                    value += dot(self.turned[tile(z + 4, 256), :], source[256:512, columns])
            value = value.astype(BF16).reshape(2, 2, 2, rows, width)
            self.weights[unit][z, :, :, :, row : row + rows, columns] = value

        loop(4, some)

    def pack_sums(self):
        small = self.weights[0]
        line = lax.broadcasted_iota(jnp.int32, (16, 128), 0)
        for group in range(8):
            block = self.sums[:, group * 128 : (group + 1) * 128]
            for k in range(4):
                first = (group * 4 + k) * 128
                feed = jnp.broadcast_to(self.feed_sum[0:1, first : first + 128], (16, 128))
                small[group // 2, group % 2, k // 2, k % 2] = jnp.where(line == 13, feed, block).astype(BF16)


def forward_steps(layer, gather):
    ready = {}
    for number, (unit, start, width, _) in enumerate(gather):
        ready.setdefault(unit, []).append((number, start, width))
    steps = [(ready[0][-1][0], 0.5, layer.unpack)]
    for number, start, width in ready[1]:
        steps.append((number, 0.7, functools.partial(layer.project, start, width)))
    memory = [(n, 1.2, functools.partial(layer.project_memory, s, w)) for n, s, w in ready[4]]
    done = ready[1][-1][0]
    for k in range(4):
        steps.append((done, 3.0, functools.partial(layer.attend, False, k // 2, (k % 2 * 4, k % 2 * 4 + 4))))
        if k < len(memory):
            steps.append(memory[k])
    steps += memory[4:]
    for number, start, width in ready[2]:
        steps.append((number, 0.7, functools.partial(layer.output, 2, layer.mixed, layer.hidden, 2, start, width)))
    steps.append((0, 1.5, functools.partial(layer.norm, 0, layer.first)))
    for number, start, width in ready[3]:
        steps.append((number, 0.7, functools.partial(layer.query, start, width)))
    for k in range(8):
        steps.append((0, 3.0, functools.partial(layer.attend, True, k // 4, (k % 4 * 2, k % 4 * 2 + 2))))
    for number, start, width in ready[5]:
        steps.append((number, 0.7, functools.partial(layer.output, 5, layer.mixed2, layer.first, 5, start, width)))
    steps.append((0, 1.5, functools.partial(layer.norm, 1, layer.second)))
    for number, start, width in ready[6]:
        steps.append((number, 1.5, functools.partial(layer.feed_up, start, width)))
    last = ready[7]
    for (_, start, width), (number, _, more) in zip(last[::2], last[1::2]):
        steps.append(
            (number, 0.8, functools.partial(layer.output, 7, layer.act, layer.second, 6, start, width + more))
        )
    return steps


def backward_steps(layer, give_out):
    part = functools.partial
    steps = [(7, 0.6, part(layer.feed_down_back, k)) for k in range(8)]
    steps.append((6, 2.5, part(layer.back, 6, layer.slope, layer.acc, True)))
    steps.append((6, 1.5, part(layer.norm_back, 1, layer.b_odd)))
    steps.append((5, 0.0, give_out.wait))
    steps.append((5, 1.0, part(layer.back, 5, layer.b_odd, layer.do, False)))
    for k in range(8):
        steps.append((4, 4.0, part(layer.attend_back, True, k // 4, (k % 4 * 2, k % 4 * 2 + 2))))
    steps.append((3, 1.0, part(layer.back, 3, layer.q2, layer.acc, True)))
    steps.append((3, 0.3, part(layer.total, 3, layer.q2, slice(0, D))))
    steps.append((3, 1.5, part(layer.norm_back, 0, layer.b_even)))
    steps.append((2, 1.0, part(layer.back, 2, layer.b_even, layer.do, False)))
    for k in range(4):
        steps.append((1, 4.0, part(layer.attend_back, False, k // 2, (k % 2 * 4, k % 2 * 4 + 4))))
    steps.append((1, 0.3, part(layer.total, 0, layer.qkv, slice(0, D))))
    steps.append((1, 0.3, part(layer.total, 1, layer.qkv, slice(2 * D, 3 * D))))
    return steps


def layer_kernel(gather, scatter, scale, names, keys, *refs):
    units = len(BLOCKS)
    own, refs = refs[:units], refs[units:]
    hidden_in, memory_in, cot_in, dec_ref, mem_ref = refs[:5]
    block_out, grad_hidden, grad_memory = refs[5:8]
    outs, refs = refs[8 : 8 + units], refs[8 + units :]
    weights, refs = refs[:units], refs[units:]
    arrays, refs = dict(zip(names, refs[: len(names)])), refs[len(names) :]
    buffers, refs = refs[: len(keys)], refs[len(keys) :]
    gather_send, gather_recv, scatter_send, scatter_recv, own_sem, credit = refs
    layer = Layer(dict(arrays, weights=weights), dec_ref, mem_ref)

    place = my_place()
    loads = [
        pltpu.make_async_copy(own[unit], weights[unit].at[block_at(place, "")], own_sem.at[unit])
        for unit in range(units)
    ]
    pairs = ((hidden_in, layer.hidden), (memory_in, layer.mem), (cot_in, layer.do))
    loads += [pltpu.make_async_copy(*pair, own_sem.at[units + k]) for k, pair in enumerate(pairs)]
    for load in loads:
        load.start()
    greet(place)

    chunks = [
        Gather(place, own[unit], weights[unit], start, width, order, number, gather_send, gather_recv)
        for number, (unit, start, width, order) in enumerate(gather)
    ]
    steps = forward_steps(layer, gather)
    loaded = set()

    def load_of(number):
        if number not in loaded:
            loaded.add(number)
            loads[number].wait()

    for number, stage in schedule(len(chunks), 5, LAG):
        if stage == 1:
            load_of(gather[number][0])
        chunks[number].stage(stage)
        if stage == 4:
            if number == 0:
                for k in range(3):
                    load_of(units + k)
            spent = 0.0
            while steps and steps[0][0] <= number and spent < FORWARD_SHARE:
                _, cost, step = steps.pop(0)
                step()
                spent += cost
    for _, _, step in steps:
        step()
    layer.last_norm()
    for chunk in chunks:
        chunk.drain()
    give_out = pltpu.make_async_copy(layer.do, block_out, own_sem.at[units])
    give_out.start()
    give_memory = pltpu.make_async_copy(layer.mem, grad_memory, own_sem.at[units + 1])
    give_hidden = pltpu.make_async_copy(layer.hidden, grad_hidden, own_sem.at[units + 2])

    rings = Rings(place, keys, buffers, credit, scatter)
    chunks = [
        Scatter(place, rings, weights[piece[0]], outs[piece[0]], scale, piece, number, scatter_send, scatter_recv)
        for number, piece in enumerate(scatter)
    ]
    steps = backward_steps(layer, give_out)
    rank = {unit: k for k, unit in enumerate(SCATTER_UNITS)}
    sources = {
        7: layer.b_even,
        6: layer.slope,
        5: layer.b_odd,
        4: layer.kv2,
        3: layer.q2,
        2: layer.b_even,
        1: layer.qkv,
    }
    begun = set()

    def begin(unit):
        if unit == 7:
            layer.turn_feed()
        elif unit == 0:
            layer.pack_sums()
        else:
            layer.turn({6: layer.second, 5: layer.mixed2, 4: layer.mem, 3: layer.first, 2: layer.mixed, 1: layer.hidden}[unit])
        if unit == 4:
            layer.back(4, layer.kv2, layer.mem, False)
            layer.total(4, layer.kv2, slice(D, 2 * D))
            give_memory.start()
        if unit == 1:
            layer.back(1, layer.qkv, layer.hidden, True)
            give_hidden.start()

    for number, stage in schedule(len(chunks), 5, LAG):
        if stage == 0:
            unit = scatter[number][0]
            while steps and rank[steps[0][0]] <= rank[unit]:
                steps.pop(0)[2]()
            if unit not in begun:
                begun.add(unit)
                begin(unit)
            if unit:
                layer.outer(unit, sources[unit], scatter[number])
        chunks[number].stage(stage)
        if stage == 0:
            spent = 0.0
            while steps and spent < BACKWARD_SHARE and (steps[0][0] != 3 or rank[unit] > 0):
                _, cost, step = steps.pop(0)
                step()
                spent += cost
    for chunk in chunks:
        chunk.drain()
    give_memory.wait()
    give_hidden.wait()


def ordered(plan, order):
    return [piece for unit in order for piece in plan if piece[0] == unit]


def layer_call(hidden_in, memory, dec_lengths, mem_lengths, cotangent, owned, scale):
    units = len(BLOCKS)
    gather = gather_plan(GATHER_UNITS, 32 * WIDTH)
    scatter = scatter_plan(SCATTER_UNITS, WIDTH)
    keys = ring_keys()
    arrays = {
        "vec": ((16, D), F32),
        "feed": ((8, FF), F32),
        "sums": ((16, D), F32),
        "feed_sum": ((8, FF), F32),
        "hidden": ((ROWS, D), BF16),
        "mem": ((KEYS, D), BF16),
        "qkv": ((ROWS, 3 * D), BF16),
        "mixed": ((ROWS, D), BF16),
        "xhat": ((2, ROWS, D), BF16),
        "inv": ((2, ROWS, 128), F32),
        "first": ((ROWS, D), BF16),
        "q2": ((ROWS, D), BF16),
        "kv2": ((KEYS, 2 * D), BF16),
        "mixed2": ((ROWS, D), BF16),
        "second": ((ROWS, D), BF16),
        "act": ((ROWS, FF), BF16),
        "slope": ((ROWS, FF), BF16),
        "turned": ((2 * D, 256), BF16),
        "turned_feed": ((32, 128, 256), BF16),
        "g": ((ROWS, D), F32),
        "acc": ((ROWS, D), F32),
        "b_even": ((ROWS, D), BF16),
        "b_odd": ((ROWS, D), BF16),
        "do": ((ROWS, D), BF16),
    }
    any_spec = pl.BlockSpec(memory_space=pl.ANY)
    vmem = pl.BlockSpec(memory_space=pltpu.VMEM)
    smem = pl.BlockSpec(memory_space=pltpu.SMEM)
    dma = pltpu.SemaphoreType.DMA
    return pl.pallas_call(
        functools.partial(layer_kernel, gather, scatter, scale, tuple(arrays), keys),
        out_shape=[jax.ShapeDtypeStruct(a.shape, BF16) for a in (hidden_in, hidden_in, memory)]
        + [jax.ShapeDtypeStruct(block, F32) for block in BLOCKS],
        in_specs=[any_spec] * (units + 3) + [smem] * 2,
        out_specs=[any_spec] * 3 + [vmem] * units,
        scratch_shapes=[pltpu.VMEM((4, 2, 2, 2, *block), BF16) for block in BLOCKS]
        + [pltpu.VMEM(*array) for array in arrays.values()]
        + [pltpu.VMEM(ring_shape(key, WIDTH), BF16) for key in keys]
        + [dma((len(gather), 6))] * 2
        + [dma((len(scatter), 6))] * 2
        + [dma((units + 3,)), pltpu.SemaphoreType.REGULAR((len(keys), 6))],
        compiler_params=pltpu.CompilerParams(collective_id=0, has_side_effects=True, vmem_limit_bytes=VMEM_LIMIT),
        name="decoder_layer",
    )(*owned, hidden_in, memory, cotangent, dec_lengths, mem_lengths)


def gelu_tanh(value):
    inner = gelu_coef * (value + 0.044715 * value * value * value)
    return 0.5 * value * (1.0 + jnp.tanh(inner))


def gelu_slope(value):
    inner = gelu_coef * (value + 0.044715 * value * value * value)
    tangent = jnp.tanh(inner)
    return 0.5 * (1.0 + tangent) + 0.5 * value * (1.0 - tangent * tangent) * gelu_coef * (
        1.0 + 3.0 * 0.044715 * value * value
    )


def product(rows_mat, weight):
    return jnp.dot(rows_mat, weight, preferred_element_type=F32)


def times_trans(rows_mat, weight):
    return jnp.einsum("tj,ij->ti", rows_mat, weight, preferred_element_type=F32)


def outer_sum(left_rows, right_rows):
    return jnp.einsum("ti,tj->ij", left_rows, right_rows, preferred_element_type=F32)


def column_total(rows_mat):
    return jnp.sum(rows_mat.astype(F32), 0)


def layer_norm(resid, gain, shift):
    center = resid - jnp.mean(resid, -1, keepdims=True)
    inv_dev = lax.rsqrt(jnp.mean(center * center, -1, keepdims=True) + epsilon)
    scaled = center * inv_dev
    return (scaled * gain + shift, scaled, inv_dev)


def norm_back(grad_out, scaled, inv_dev, gain):
    grad_scaled = grad_out * gain
    grad_resid = inv_dev * (
        grad_scaled
        - jnp.mean(grad_scaled, -1, keepdims=True)
        - scaled * jnp.mean(grad_scaled * scaled, -1, keepdims=True)
    )
    return (grad_resid, jnp.sum(grad_out * scaled, 0), jnp.sum(grad_out, 0))


def split_heads(matrix, length):
    return matrix.reshape(-1, length, HEADS, HEAD_DIM)


def merge_heads(tensor):
    return tensor.reshape(-1, D)


def scores_of(query_rows, key_rows, allowed):
    keys = allowed.shape[-1]
    raw = jnp.einsum(
        "sqhe,skhe->shqk",
        split_heads(query_rows, DEC),
        split_heads(key_rows, keys),
        preferred_element_type=F32,
    )
    return jnp.where(allowed[:, None], raw * HEAD_DIM ** (-0.5), -1000000000.0)


def attend(query_rows, key_rows, value_rows, allowed):
    scores = scores_of(query_rows, key_rows, allowed)
    top_score = jnp.max(scores, -1, keepdims=True)
    log_total = top_score + jnp.log(jnp.sum(jnp.exp(scores - top_score), -1, keepdims=True))
    probabilities = jnp.exp(scores - log_total).astype(BF16)
    mixed = jnp.einsum(
        "shqk,skhe->sqhe",
        probabilities,
        split_heads(value_rows, allowed.shape[-1]),
        preferred_element_type=F32,
    )
    return (merge_heads(mixed).astype(BF16), log_total)


def attend_back(query_rows, key_rows, value_rows, allowed, log_total, grad_mixed):
    keys = allowed.shape[-1]
    probabilities = jnp.exp(scores_of(query_rows, key_rows, allowed) - log_total)
    grad_heads = split_heads(grad_mixed, DEC)
    grad_value = jnp.einsum(
        "shqk,sqhe->skhe", probabilities.astype(BF16), grad_heads, preferred_element_type=F32
    )
    grad_probs = jnp.einsum(
        "sqhe,skhe->shqk", grad_heads, split_heads(value_rows, keys), preferred_element_type=F32
    )
    grad_scores = probabilities * (
        grad_probs - jnp.sum(probabilities * grad_probs, -1, keepdims=True)
    )
    grad_raw = (grad_scores * HEAD_DIM ** (-0.5)).astype(BF16)
    grad_query = jnp.einsum(
        "shqk,skhe->sqhe", grad_raw, split_heads(key_rows, keys), preferred_element_type=F32
    )
    grad_key = jnp.einsum(
        "shqk,sqhe->skhe", grad_raw, split_heads(query_rows, DEC), preferred_element_type=F32
    )
    return (
        merge_heads(grad_query).astype(BF16),
        merge_heads(grad_key).astype(BF16),
        merge_heads(grad_value).astype(BF16),
    )


def masks_for(dec_lengths, mem_lengths):
    row_ids = jnp.arange(DEC)
    inside = row_ids[None, :] < dec_lengths[:, None]
    valid_rows = inside.reshape(-1, 1)
    causal = (row_ids[None, None, :] <= row_ids[None, :, None]) & inside[:, None, :]
    mem_seen = (jnp.arange(MEM)[None, :] < mem_lengths[:, None])[:, None, :]
    mem_seen = jnp.broadcast_to(mem_seen, (mem_lengths.shape[0], DEC, MEM))
    return (valid_rows, causal, mem_seen)


def run_forward(weights, hidden, mem_rows, dec_lengths, mem_lengths):
    (
        self_project,
        self_output,
        cross_query,
        cross_memory,
        cross_output,
        feed_in,
        feed_out,
        bias_rows,
        feed_bias,
        norm_gains,
        norm_shifts,
    ) = weights
    bias_full = bias_rows.astype(F32)
    gain_full = norm_gains.astype(F32)
    shift_full = norm_shifts.astype(F32)
    valid_rows, causal, mem_seen = masks_for(dec_lengths, mem_lengths)
    projected = product(hidden, self_project)
    query_rows = (projected[:, :D] + bias_full[0]).astype(BF16)
    key_rows = projected[:, D : 2 * D].astype(BF16)
    value_rows = (projected[:, 2 * D :] + bias_full[1]).astype(BF16)
    mixed, log_one = attend(query_rows, key_rows, value_rows, causal)
    resid_one = alpha_res * hidden.astype(F32) + product(mixed, self_output) + bias_full[2]
    first, scaled_one, inv_one = layer_norm(resid_one, gain_full[0], shift_full[0])
    first = first.astype(BF16)
    cross_q = (product(first, cross_query) + bias_full[3]).astype(BF16)
    mem_proj = product(mem_rows, cross_memory)
    cross_k = mem_proj[:, :D].astype(BF16)
    cross_v = (mem_proj[:, D:] + bias_full[4]).astype(BF16)
    mixed_two, log_two = attend(cross_q, cross_k, cross_v, mem_seen)
    resid_two = (
        alpha_res * first.astype(F32) + product(mixed_two, cross_output) + bias_full[5]
    )
    second, scaled_two, inv_two = layer_norm(resid_two, gain_full[1], shift_full[1])
    second = second.astype(BF16)
    pre_act = product(second, feed_in) + feed_bias.astype(F32)
    active = gelu_tanh(pre_act).astype(BF16)
    resid_three = alpha_res * second.astype(F32) + product(active, feed_out) + bias_full[6]
    normed, scaled_three, inv_three = layer_norm(resid_three, gain_full[2], shift_full[2])
    block_out = jnp.where(valid_rows, normed, 0.0).astype(BF16)
    saved = (
        query_rows,
        key_rows,
        value_rows,
        log_one,
        mixed,
        scaled_one,
        inv_one,
        first,
        cross_q,
        cross_k,
        cross_v,
        log_two,
        mixed_two,
        scaled_two,
        inv_two,
        second,
        pre_act,
        active,
        scaled_three,
        inv_three,
    )
    return (saved, block_out)


def run_backward(weights, saved, hidden, mem_rows, cot_rows, dec_lengths, mem_lengths):
    (
        self_project,
        self_output,
        cross_query,
        cross_memory,
        cross_output,
        feed_in,
        feed_out,
        bias_rows,
        feed_bias,
        norm_gains,
        norm_shifts,
    ) = weights
    (
        query_rows,
        key_rows,
        value_rows,
        log_one,
        mixed,
        scaled_one,
        inv_one,
        first,
        cross_q,
        cross_k,
        cross_v,
        log_two,
        mixed_two,
        scaled_two,
        inv_two,
        second,
        pre_act,
        active,
        scaled_three,
        inv_three,
    ) = saved
    gain_full = norm_gains.astype(F32)
    valid_rows, causal, mem_seen = masks_for(dec_lengths, mem_lengths)
    grad_top = jnp.where(valid_rows, cot_rows.astype(F32), 0.0)
    grad_three, gain_three, shift_three = norm_back(grad_top, scaled_three, inv_three, gain_full[2])
    branch_three = grad_three.astype(BF16)
    grad_feed_out = outer_sum(active, branch_three)
    grad_pre = (times_trans(branch_three, feed_out) * gelu_slope(pre_act)).astype(BF16)
    grad_feed_in = outer_sum(second, grad_pre)
    grad_second = (alpha_res * grad_three + times_trans(grad_pre, feed_in)).astype(BF16)
    grad_two, gain_two, shift_two = norm_back(
        grad_second.astype(F32), scaled_two, inv_two, gain_full[1]
    )
    branch_two = grad_two.astype(BF16)
    grad_cross_output = outer_sum(mixed_two, branch_two)
    grad_mixed_two = times_trans(branch_two, cross_output).astype(BF16)
    grad_cq, grad_ck, grad_cv = attend_back(
        cross_q, cross_k, cross_v, mem_seen, log_two, grad_mixed_two
    )
    grad_mem_proj = jnp.concatenate([grad_ck, grad_cv], 1)
    grad_cross_memory = outer_sum(mem_rows, grad_mem_proj)
    grad_mem_rows = times_trans(grad_mem_proj, cross_memory).astype(BF16)
    grad_cross_query = outer_sum(first, grad_cq)
    grad_first = (alpha_res * grad_two + times_trans(grad_cq, cross_query)).astype(BF16)
    grad_one, gain_one, shift_one = norm_back(
        grad_first.astype(F32), scaled_one, inv_one, gain_full[0]
    )
    branch_one = grad_one.astype(BF16)
    grad_self_output = outer_sum(mixed, branch_one)
    grad_mixed = times_trans(branch_one, self_output).astype(BF16)
    grad_q, grad_k, grad_v = attend_back(
        query_rows, key_rows, value_rows, causal, log_one, grad_mixed
    )
    grad_projected = jnp.concatenate([grad_q, grad_k, grad_v], 1)
    grad_self_project = outer_sum(hidden, grad_projected)
    grad_hidden = (alpha_res * grad_one + times_trans(grad_projected, self_project)).astype(
        BF16
    )
    grad_bias_rows = jnp.stack(
        [
            column_total(grad_q),
            column_total(grad_v),
            column_total(branch_one),
            column_total(grad_cq),
            column_total(grad_cv),
            column_total(branch_two),
            column_total(branch_three),
        ]
    )
    grads = (
        grad_self_project,
        grad_self_output,
        grad_cross_query,
        grad_cross_memory,
        grad_cross_output,
        grad_feed_in,
        grad_feed_out,
        grad_bias_rows,
        column_total(grad_pre),
        jnp.stack([gain_one, gain_two, gain_three]),
        jnp.stack([shift_one, shift_two, shift_three]),
    )
    return (grads, grad_hidden, grad_mem_rows)


SMALL = 13


def pack_small(bias_rows, feed_bias, norm_gains, norm_shifts):
    rows = jnp.concatenate([bias_rows, norm_gains, norm_shifts], 0)
    span = rows.shape[1]
    lane = lax.broadcasted_iota(jnp.int32, (SMALL, 128), 1) // span
    rows = jnp.where(lane == lax.axis_index("shard"), jnp.tile(rows, (1, 128 // span)), 0)
    rest = jnp.zeros((2, 128), BF16)
    return jnp.concatenate([rows, feed_bias[None], rest], 0)


def unpack_small_grads(block):
    rows = lax.dynamic_slice_in_dim(block[:SMALL], lax.axis_index("shard") * 32, 32, 1)
    return rows[:7], block[SMALL], rows[7:10], rows[10:]


def gather_by_collectives(owned):
    axis = [0] * 7 + [1, 0, 1, 1]
    return tuple(lax.all_gather(a, AXES, axis=d, tiled=True) for a, d in zip(owned, axis))


def scatter_by_collectives(grads, factor):
    axis = [0] * 7 + [1, 0, 1, 1]
    return tuple(
        lax.psum_scatter(a * factor, AXES, scatter_dimension=d, tiled=True) for a, d in zip(grads, axis)
    )


def body(by_kernel, hidden_in, memory, dec_lengths, mem_lengths, cotangent, *owned):
    token_count = hidden_in.shape[0] * lax.axis_size(AXES)
    factor = float(token_count) ** (-0.5)
    if by_kernel:
        packed = (pack_small(*owned[7:]), *owned[:7])
        block_out, grad_hidden, grad_memory, *shares = layer_call(
            hidden_in, memory, dec_lengths, mem_lengths, cotangent, packed, factor
        )
        return (block_out, grad_hidden, grad_memory, *shares[1:], *unpack_small_grads(shares[0]))
    weights = gather_by_collectives(owned)
    saved, block_out = run_forward(weights, hidden_in, memory, dec_lengths, mem_lengths)
    grads, grad_hidden, grad_memory = run_backward(
        weights, saved, hidden_in, memory, cotangent, dec_lengths, mem_lengths
    )
    return (block_out, grad_hidden, grad_memory, *scatter_by_collectives(grads, factor))


def solution(mesh):
    rows, columns, vector = P(AXES, None), P(None, AXES), P(AXES)
    in_specs = (rows, rows, vector, vector, rows, *[rows] * 7, columns, vector, columns, columns)
    out_specs = (rows, rows, rows, *[rows] * 7, columns, vector, columns, columns)
    by_kernel = mesh.shape["dp"] == 8 and mesh.shape["shard"] == 4
    return jax.shard_map(
        functools.partial(body, by_kernel), mesh=mesh, in_specs=in_specs, out_specs=out_specs, check_vma=False
    )
```

```python
import functools
import math

import jax
import jax.numpy as jnp
from jax import lax
from jax.experimental import pallas as pl
from jax.experimental.pallas import tpu as pltpu
from jax.sharding import PartitionSpec as P

D = 1024
HEADS = 16
HEAD_DIM = 64
DEC = 128
MEM = 256
AXES = ("dp", "shard")
MESH_ID = pl.DeviceIdType.MESH
BF16 = jnp.bfloat16
F32 = jnp.float32

alpha_res = 300.0**0.25
epsilon = 1e-05
gelu_coef = math.sqrt(2.0 / math.pi)

SIZES = {"z": 4, "x": 2, "y": 2}
FF = 4096
LAG = 3
WINDOW = 24
SLOTS = {"s": 4}
FORWARD_SHARE = 4.0
BACKWARD_SHARE = 1.0
ABREAST = 2
VMEM_LIMIT = 62 * 2**20
WIDTH = 512
GATHER_ORDERS = ("zxy", "xzy", "zyx", "yzx", "xzy", "yzx")
SCATTER_ORDERS = ("yxz", "yzx", "xyz", "xzy", "yzx", "xzy")


def my_place():
    dp, shard = lax.axis_index("dp"), lax.axis_index("shard")
    place = {
        "z": lax.div(dp, 2),
        "x": lax.rem(dp, 2),
        "y": lax.div(shard, 2),
        "c": lax.rem(shard, 2),
    }
    z = place["z"]
    place["middle"] = (z == 1) | (z == 2)
    place["end"] = (z == 0) | (z == 3)
    place["pair"] = z + 1 - 2 * lax.rem(z, 2)
    place["far"] = 2 - 2 * lax.div(z, 2)
    place["across"] = 2 - lax.div(z, 2)
    place["beyond"] = 3 - 3 * lax.div(z, 2)
    return place


def device_of(place):
    return (place["z"] * 2 + place["x"], place["y"] * 2 + place["c"])


def moved(place, **changes):
    return {**place, **changes}


def across(place, dim):
    key = "c" if dim == "s" else dim
    return moved(place, **{key: 1 - place[key]})


def greet(place):
    barrier = pltpu.get_barrier_semaphore()
    others = [across(place, dim) for dim in "xys"]
    others += [moved(place, z=lax.rem(place["z"] + k, 4)) for k in (1, 2, 3)]
    for other in others:
        pl.semaphore_signal(barrier, inc=1, device_id=device_of(other), device_id_type=MESH_ID)
    pl.semaphore_wait(barrier, len(others))


def block_at(place, whole):
    return tuple(pl.ds(0, SIZES.get(d, 2)) if d in whole else place[d] for d in ("z", "x", "y", "c"))


def when(condition, action):
    if condition is True:
        action()
    else:
        pl.when(condition)(action)


class Mover:
    def __init__(self, place, number, send_sem, recv_sem):
        self.place, self.number = place, number % WINDOW
        self.send_sem, self.recv_sem = send_sem, recv_sem
        self.waiting = []

    def move(self, source, target, slot, other, sends=True, receives=True):
        copy = pltpu.make_async_remote_copy(
            src_ref=source,
            dst_ref=target,
            send_sem=self.send_sem.at[self.number, slot],
            recv_sem=self.recv_sem.at[self.number, slot],
            device_id=device_of(other),
            device_id_type=MESH_ID,
        )
        when(sends, copy.start)
        self.waiting.append((copy, sends, receives))

    def settle(self):
        for copy, sends, receives in self.waiting:
            when(receives, copy.wait_recv)
            when(sends, copy.wait_send)
        self.waiting = []


SLOT = {"x": 0, "y": 1, "s": 2}


class Gather(Mover):
    def __init__(self, place, own, full, start, width, order, number, send_sem, recv_sem):
        super().__init__(place, number, send_sem, recv_sem)
        self.own, self.full = own, full
        self.columns = pl.ds(start, width)
        self.path, held = [], ""
        for dim in order + "s":
            self.path += [(step, held) for step in (("near", "on") if dim == "z" else dim)]
            held += dim

    def part(self, index):
        return self.full.at[(*index, slice(None), self.columns)]

    def stage(self, number):
        self.settle()
        if number == GATHER_STAGES - 1:
            return
        dim, held = self.path[number]
        place = self.place
        index = block_at(place, held)
        target = self.part(index)
        source = target if number else self.own.at[:, self.columns]
        if dim == "near":
            self.move(source, target, 3, moved(place, z=place["pair"]))
            for slot, sends in ((4, place["end"]), (5, place["middle"])):
                self.move(source, target, slot, moved(place, z=place["across"]), sends, place["middle"])
        elif dim == "on":
            both = self.part((pl.ds(place["far"], 2), *index[1:]))
            self.move(both, both, 4, moved(place, z=place["pair"]), place["middle"], place["end"])
        else:
            self.move(source, target, SLOT[dim], across(place, dim))


GATHER_STAGES = 6
SCATTER_STAGES = 6


def schedule(count, stages, lag):
    for step in range(count + (stages - 1) * lag):
        for stage in reversed(range(stages)):
            if 0 <= step - stage * lag < count:
                yield step - stage * lag, stage


def gather_plan(units, size):
    plan = []
    for unit in units:
        rows, columns = BLOCKS[unit]
        width = min(columns, size // rows)
        for start in range(0, columns, width):
            plan.append((unit, start, width, GATHER_ORDERS[len(plan) % len(GATHER_ORDERS)]))
    return plan


def rings_of(order):
    keys = [("s", "zxy")]
    left = "zxy"
    for dim in order:
        left = left.replace(dim, "")
        keys += [("fold", left), ("share", left)] if dim == "z" else [(dim, left)]
    return keys


def slots_of(key):
    return SLOTS.get(key[0], 3)


def ring_shape(key, width):
    step, left = key
    return (slots_of(key), 2 if step in ("fold", "share") else 1, *[SIZES[d] for d in left], 32, width)


class Rings:
    def __init__(self, place, keys, buffers, credit, plan):
        self.place, self.credit = place, credit
        self.number = {key: k for k, key in enumerate(keys)}
        self.buffer = dict(zip(keys, buffers))
        users = {key: [] for key in keys}
        for number, piece in enumerate(plan):
            for key in rings_of(piece[5]):
                users[key].append(number)
        for key, numbers in users.items():
            slots = slots_of(key)
            assert all(b - a >= LAG for a, b in zip(numbers, numbers[slots:]))
        self.uses = {key: len(numbers) for key, numbers in users.items()}
        self.turn = {key: 0 for key in keys}

    def links(self, key):
        step, place = key[0], self.place
        pair = moved(place, z=place["pair"])
        if step == "fold":
            return [(0, place["end"], pair, place["middle"])]
        if step == "share":
            other = moved(place, z=place["across"])
            return [
                (1, True, pair, True),
                (2, place["middle"], other, place["middle"]),
                (3, place["middle"], other, place["end"]),
            ]
        return [(0, True, across(place, step), True)]

    def take(self, key):
        turn = self.turn[key]
        self.turn[key] += 1
        if turn >= slots_of(key):
            for slot, sends, _, _ in self.links(key):
                when(sends, functools.partial(pl.semaphore_wait, self.credit.at[self.number[key], slot], 1))
        return turn % slots_of(key)

    def give(self, key):
        self.given = getattr(self, "given", {})
        turn = self.given[key] = self.given.get(key, -1) + 1
        if turn + slots_of(key) >= self.uses[key]:
            return
        for slot, _, other, receives in self.links(key):
            when(
                receives,
                functools.partial(
                    pl.semaphore_signal,
                    self.credit.at[self.number[key], slot],
                    inc=1,
                    device_id=device_of(other),
                    device_id_type=MESH_ID,
                ),
            )


class Scatter(Mover):
    def __init__(self, place, rings, grads, out, scale, piece, number, send_sem, recv_sem):
        super().__init__(place, number, send_sem, recv_sem)
        _, row, rows, start, width, order = piece
        self.rings, self.grads, self.out, self.scale = rings, grads, out, scale
        self.part = (pl.ds(row, rows), pl.ds(start, width))
        self.corner = (pl.ds(0, rows), pl.ds(0, width))
        self.keys = rings_of(order)

    def send(self, stage):
        key = self.keys[stage]
        step, left = key
        place = self.place
        self.slot = self.rings.take(key)
        buffer = self.rings.buffer[key]
        inner = [slice(None)] * len(left)

        def mine(place):
            return self.grads.at[(*block_at(place, left), *self.part)]

        if step == "fold":
            index = block_at(place, left)
            source = self.grads.at[(pl.ds(place["far"], 2), *index[1:], *self.part)]
            target = buffer.at[(self.slot, slice(None), *inner, *self.corner)]
            self.move(source, target, 5, moved(place, z=place["pair"]), place["end"], place["middle"])
        elif step == "share":
            targets = [buffer.at[(self.slot, k, *inner, *self.corner)] for k in (0, 1)]
            pair, middle, end = (moved(place, z=place[d]) for d in ("pair", "across", "beyond"))
            self.move(mine(pair), targets[0], 3, pair)
            self.move(mine(middle), targets[1], 4, middle, place["middle"], place["middle"])
            self.move(mine(end), targets[1], 5, end, place["middle"], place["end"])
        else:
            other = across(place, step)
            self.move(mine(other), buffer.at[(self.slot, 0, *inner, *self.corner)], SLOT[step], other)

    def add(self, stage):
        key = self.keys[stage]
        step, left = key
        place = self.place
        self.settle()
        buffer = self.rings.buffer[key]

        def fold(index, inner, count=1, first=0):
            value = self.grads[(*index, *self.part)].astype(F32)
            for k in range(first, first + count):
                value += buffer[(self.slot, k, *inner, *self.corner)].astype(F32)
            return value

        def add_all():
            if step == "fold":
                for k in (0, 1):
                    index = block_at(moved(place, z=place["far"] + k), left)
                    inner = (slice(None),) * len(left)
                    self.grads[(*index, *self.part)] = fold(index, inner, 1, k).astype(BF16)
                return
            count = 2 if step == "share" else 1
            if not left:
                self.out[self.part] = fold(block_at(place, left), (), count) * self.scale
                return
            first, rest = left[0], left[1:]

            def body(i, _):
                index = block_at(moved(place, **{first: i}), rest)
                inner = (i, *[slice(None)] * len(rest))
                self.grads[(*index, *self.part)] = fold(index, inner, count).astype(BF16)
                return 0

            lax.fori_loop(0, SIZES[first], body, 0)

        when(place["middle"] if step == "fold" else True, add_all)
        self.rings.give(key)

    def stage(self, number):
        if number > 0:
            self.add(number - 1)
        if number < SCATTER_STAGES - 1:
            self.send(number)


def scatter_plan(units, width):
    plan = []
    for unit in units:
        rows, columns = BLOCKS[unit]
        for row in range(0, rows, 32):
            for start in range(0, columns, width):
                order = SCATTER_ORDERS[len(plan) % len(SCATTER_ORDERS)]
                plan.append((unit, row, min(rows, 32), start, min(columns, width), order))
    return plan


def ring_keys():
    return sorted({key for order in SCATTER_ORDERS for key in rings_of(order)})


BLOCKS = ((16, 128), (32, 3 * D), (32, D), (32, D), (32, 2 * D), (32, D), (32, FF), (128, D))
GATHER_UNITS = (0, 1, 4, 2, 3, 5, 6, 7)
SCATTER_UNITS = (7, 6, 5, 4, 3, 2, 1, 0)
ROWS = 2 * DEC
KEYS = 2 * MEM


def dot(left, right):
    return jnp.dot(left, right, preferred_element_type=F32)


def dot_rows(left, right):
    return lax.dot_general(left, right, (((1,), (1,)), ((), ())), preferred_element_type=F32)


def dot_columns(left, right):
    return lax.dot_general(left, right, (((0,), (0,)), ((), ())), preferred_element_type=F32)


def flat(value):
    return value.reshape(-1, value.shape[-1])


def tile(index, size):
    return pl.ds(pl.multiple_of(index * size, size), size)


def loop(count, body):
    def step(i, carry):
        body(i)
        return carry

    lax.fori_loop(0, count, step, 0)


class Layer:
    def __init__(self, refs, dec_ref, mem_ref):
        self.dec_ref, self.mem_ref = dec_ref, mem_ref
        self.__dict__.update(refs)

    def unpack(self):
        small = self.weights[0]
        for group in range(8):
            block = small[group // 2, group % 2].astype(F32)
            self.vec[:, group * 128 : (group + 1) * 128] = block[0, 0] + block[0, 1] + block[1, 0] + block[1, 1]
            for k in range(4):
                first = (group * 4 + k) * 128
                self.feed[0:1, first : first + 128] = block[k // 2, k % 2, 13:14]
        self.sums[...] = jnp.zeros_like(self.sums)

    def row(self, number, columns=slice(None)):
        return self.vec[number : number + 1, columns]

    def project(self, start, width):
        out = dot(self.hidden[...], flat(self.weights[1][..., start : start + width]))
        if start < D:
            out += self.row(0, slice(start, start + width))
        elif start >= 2 * D:
            out += self.row(1, slice(start - 2 * D, start - 2 * D + width))
        self.qkv[:, start : start + width] = out.astype(BF16)

    def project_memory(self, start, width):
        weight = flat(self.weights[4][..., start : start + width])

        def half(i):
            out = dot(self.mem[tile(i, 256), :], weight)
            if start >= D:
                out += self.row(4, slice(start - D, start - D + width))
            self.kv2[tile(i, 256), start : start + width] = out.astype(BF16)

        loop(2, half)

    def output(self, unit, source, resid, bias, start, width):
        columns = slice(start, start + width)
        out = dot(source[...], flat(self.weights[unit][..., columns])) + self.row(bias, columns)
        self.acc[:, columns] = out + alpha_res * resid[:, columns].astype(F32)

    def query(self, start, width):
        columns = slice(start, start + width)
        out = dot(self.first[...], flat(self.weights[3][..., columns])) + self.row(3, columns)
        self.q2[:, columns] = out.astype(BF16)

    def feed_up(self, start, width):
        columns = slice(start, start + width)
        pre = dot(self.second[...], flat(self.weights[6][..., columns])) + self.feed[0:1, columns]
        square = pre * pre
        tangent = jnp.tanh(gelu_coef * pre * (1.0 + 0.044715 * square))
        self.act[:, columns] = (0.5 * pre * (1.0 + tangent)).astype(BF16)
        slope = 0.5 * (1.0 + tangent) + 0.5 * pre * (1.0 - tangent * tangent) * gelu_coef * (
            1.0 + 3.0 * 0.044715 * square
        )
        self.slope[:, columns] = slope.astype(BF16)

    def standard(self, rows):
        resid = self.acc[rows, :]
        center = resid - jnp.mean(resid, -1, keepdims=True)
        inv = lax.rsqrt(jnp.mean(center * center, -1, keepdims=True) + epsilon)
        return center * inv, inv

    def norm(self, number, out):
        def some(i):
            rows = tile(i, 64)
            scaled, inv = self.standard(rows)
            self.xhat[number, rows, :] = scaled.astype(BF16)
            self.inv[number, rows, :] = jnp.broadcast_to(inv, (64, 128))
            out[rows, :] = (scaled * self.row(7 + number) + self.row(10 + number)).astype(BF16)

        loop(4, some)

    def norm_grad(self, number, grad, scaled, inv, rows, b_ref):
        grad_scaled = grad * self.row(7 + number)
        resid = inv * (
            grad_scaled
            - jnp.mean(grad_scaled, -1, keepdims=True)
            - scaled * jnp.mean(grad_scaled * scaled, -1, keepdims=True)
        )
        branch = resid.astype(BF16)
        self.g[rows, :] = resid
        b_ref[rows, :] = branch
        bias = (2, 5, 6)[number]
        self.sums[7 + number : 8 + number, :] += jnp.sum(grad * scaled, 0, keepdims=True)
        self.sums[10 + number : 11 + number, :] += jnp.sum(grad, 0, keepdims=True)
        self.sums[bias : bias + 1, :] += jnp.sum(branch.astype(F32), 0, keepdims=True)

    def last_norm(self):
        def some(i):
            rows = tile(i, 64)
            scaled, inv = self.standard(rows)
            ids = lax.broadcasted_iota(jnp.int32, (64, 1), 0) + lax.rem(i, 2) * 64
            valid = ids < self.dec_ref[lax.div(i, 2)]
            grad = jnp.where(valid, self.do[rows, :].astype(F32), 0.0)
            out = scaled * self.row(9) + self.row(12)
            self.do[rows, :] = jnp.where(valid, out, 0.0).astype(BF16)
            self.norm_grad(2, grad, scaled, inv, rows, self.b_even)

        loop(4, some)

    def norm_back(self, number, b_ref):
        def some(i):
            rows = tile(i, 64)
            grad = self.acc[rows, :].astype(BF16).astype(F32)
            scaled = self.xhat[number, rows, :].astype(F32)
            self.norm_grad(number, grad, scaled, self.inv[number, rows, 0:1], rows, b_ref)

        loop(4, some)

    def stacked(self, value):
        low = lax.broadcasted_iota(jnp.int32, (DEC, 128), 1) < HEAD_DIM
        zero = jnp.zeros_like(value)
        return jnp.concatenate([jnp.where(low, value, zero), jnp.where(low, zero, value)], 0)

    def unstacked(self, value):
        low = lax.broadcasted_iota(jnp.int32, (DEC, 128), 1) < HEAD_DIM
        return jnp.where(low, value[:DEC], value[DEC:])

    def heads(self, cross, seq, pair):
        rows = tile(seq, DEC)
        if cross:
            keys, ref, first = tile(seq, MEM), self.kv2, 0
            q_at = (self.q2, rows, tile(pair, 128))
        else:
            keys, ref, first = rows, self.qkv, 8
            q_at = (self.qkv, rows, tile(pair, 128))
        k_at = (ref, keys, tile(first + pair, 128))
        v_at = (ref, keys, tile(first + 8 + pair, 128))
        return rows, q_at, k_at, v_at

    def weights_of(self, cross, seq, queries, key_rows):
        raw = dot_rows(queries, key_rows)
        column = lax.broadcasted_iota(jnp.int32, raw.shape, 1)
        if cross:
            allowed = column < self.mem_ref[seq]
        else:
            line = lax.rem(lax.broadcasted_iota(jnp.int32, raw.shape, 0), DEC)
            allowed = (column <= line) & (column < self.dec_ref[seq])
        scores = jnp.where(allowed, raw * HEAD_DIM ** (-0.5), -1000000000.0)
        expo = jnp.exp(scores - jnp.max(scores, -1, keepdims=True))
        return expo * (1.0 / jnp.sum(expo, -1, keepdims=True))

    def attend(self, cross, seq, pairs):
        out = self.mixed2 if cross else self.mixed

        def some(i):
            held = []
            for k in range(ABREAST):
                pair = i * ABREAST + k + pairs[0]
                rows, q_at, k_at, v_at = self.heads(cross, seq, pair)
                held.append((rows, pair, *[at[0][at[1:]] for at in (q_at, k_at, v_at)]))
            mixed = []
            for _, _, queries, key_rows, value_rows in held:
                probabilities = self.weights_of(cross, seq, self.stacked(queries), key_rows)
                mixed.append(self.unstacked(dot(probabilities.astype(BF16), value_rows)).astype(BF16))
            for (rows, pair, *_), value in zip(held, mixed):
                out[rows, tile(pair, 128)] = value

        loop((pairs[1] - pairs[0]) // ABREAST, some)

    def attend_back(self, cross, seq, pairs):
        def some(i):
            held = []
            for k in range(ABREAST):
                pair = i * ABREAST + k + pairs[0]
                rows, *places = self.heads(cross, seq, pair)
                values = [at[0][at[1:]] for at in places]
                held.append((places, *values, self.do[rows, tile(pair, 128)]))
            results = []
            for _, queries, key_rows, value_rows, grads in held:
                queries, grads = self.stacked(queries), self.stacked(grads)
                probabilities = self.weights_of(cross, seq, queries, key_rows)
                grad_value = dot_columns(probabilities.astype(BF16), grads)
                grad_probs = dot_rows(grads, value_rows)
                mean = jnp.sum(probabilities * grad_probs, -1, keepdims=True)
                grad_raw = (probabilities * (grad_probs - mean) * HEAD_DIM ** (-0.5)).astype(BF16)
                grad_query = self.unstacked(dot(grad_raw, key_rows))
                grad_key = dot_columns(grad_raw, queries)
                results.append([value.astype(BF16) for value in (grad_query, grad_key, grad_value)])
            for (places, *_), values in zip(held, results):
                for at, value in zip(places, values):
                    at[0][at[1:]] = value

        loop((pairs[1] - pairs[0]) // ABREAST, some)

    def feed_down_back(self, part):
        columns = slice(part * 512, part * 512 + 512)
        grad = dot_rows(self.b_even[...], flat(self.weights[7][part // 2, part % 2]))
        grad = (grad * self.slope[:, columns].astype(F32)).astype(BF16)
        self.slope[:, columns] = grad
        self.feed_sum[0:1, columns] = jnp.sum(grad.astype(F32), 0, keepdims=True)

    def back(self, unit, source, out, resid):
        def some(z):
            columns = tile(z, 256)
            value = dot_rows(source[...], flat(self.weights[unit][z]))
            if resid:
                value += alpha_res * self.g[:, columns]
            out[:, columns] = value.astype(out.dtype)

        loop(4, some)

    def total(self, number, source, columns):
        self.sums[number : number + 1, :] = jnp.sum(source[:, columns].astype(F32), 0, keepdims=True)

    def turn(self, source):
        for k in range(source.shape[0] // 256):
            for column in range(0, D, 256):
                block = source[k * 256 : (k + 1) * 256, column : column + 256]
                first = k * D + column
                self.act[:, first : first + 256] = block.T

    def turn_feed(self):
        for k in range(8):
            block = self.act[:, k * 512 : (k + 1) * 512].T
            self.turned_feed[k * 4 : (k + 1) * 4] = block.reshape(4, 128, 256)

    def outer(self, unit, source, piece):
        _, row, rows, start, width, _ = piece
        def some(k):
            columns = pl.ds(pl.multiple_of(start + k * 256, 256), 256)
            right = source[0:256, columns]
            for z in range(4):
                if unit == 7:
                    left = flat(self.turned_feed[z * 8 : z * 8 + 8, row : row + rows, :])
                    value = dot(left, right)
                else:
                    value = dot(self.act[:, z * 256 : z * 256 + 256], right)
                    if unit == 4:
                        value += dot(self.act[:, D + z * 256 : D + z * 256 + 256], source[256:512, columns])
                value = value.astype(BF16).reshape(2, 2, 2, rows, 256)
                self.weights[unit][z, :, :, :, row : row + rows, columns] = value

        loop(width // 256, some)

    def pack_sums(self):
        small = self.weights[0]
        line = lax.broadcasted_iota(jnp.int32, (16, 128), 0)
        for group in range(8):
            block = self.sums[:, group * 128 : (group + 1) * 128]
            for k in range(4):
                first = (group * 4 + k) * 128
                feed = jnp.broadcast_to(self.feed_sum[0:1, first : first + 128], (16, 128))
                small[group // 2, group % 2, k // 2, k % 2] = jnp.where(line == 13, feed, block).astype(BF16)


def forward_steps(layer, gather):
    ready = {}
    for number, (unit, start, width, _) in enumerate(gather):
        ready.setdefault(unit, []).append((number, start, width))
    steps = [(ready[0][-1][0], 0.5, layer.unpack)]
    for number, start, width in ready[1]:
        steps.append((number, 0.7, functools.partial(layer.project, start, width)))
    memory = [(n, 1.2, functools.partial(layer.project_memory, s, w)) for n, s, w in ready[4]]
    done = ready[1][-1][0]
    for k in range(4):
        steps.append((done, 3.0, functools.partial(layer.attend, False, k // 2, (k % 2 * 4, k % 2 * 4 + 4))))
        if k < len(memory):
            steps.append(memory[k])
    steps += memory[4:]
    for number, start, width in ready[2]:
        steps.append((number, 0.7, functools.partial(layer.output, 2, layer.mixed, layer.hidden, 2, start, width)))
    steps.append((0, 1.5, functools.partial(layer.norm, 0, layer.first)))
    for number, start, width in ready[3]:
        steps.append((number, 0.7, functools.partial(layer.query, start, width)))
    for k in range(8):
        steps.append((0, 3.0, functools.partial(layer.attend, True, k // 4, (k % 4 * 2, k % 4 * 2 + 2))))
    for number, start, width in ready[5]:
        steps.append((number, 0.7, functools.partial(layer.output, 5, layer.mixed2, layer.first, 5, start, width)))
    steps.append((0, 1.5, functools.partial(layer.norm, 1, layer.second)))
    for number, start, width in ready[6]:
        steps.append((number, 1.5, functools.partial(layer.feed_up, start, width)))
    last = ready[7]
    for (_, start, width), (number, _, more) in zip(last[::2], last[1::2]):
        steps.append(
            (number, 0.8, functools.partial(layer.output, 7, layer.act, layer.second, 6, start, width + more))
        )
    return steps


def backward_steps(layer, give_out):
    part = functools.partial
    steps = [(7, 0.6, part(layer.feed_down_back, k)) for k in range(8)]
    steps.append((6, 2.5, part(layer.back, 6, layer.slope, layer.acc, True)))
    steps.append((6, 1.5, part(layer.norm_back, 1, layer.b_odd)))
    steps.append((5, 0.0, give_out.wait))
    steps.append((5, 1.0, part(layer.back, 5, layer.b_odd, layer.do, False)))
    for k in range(8):
        steps.append((4, 4.0, part(layer.attend_back, True, k // 4, (k % 4 * 2, k % 4 * 2 + 2))))
    steps.append((3, 1.0, part(layer.back, 3, layer.q2, layer.acc, True)))
    steps.append((3, 0.3, part(layer.total, 3, layer.q2, slice(0, D))))
    steps.append((3, 1.5, part(layer.norm_back, 0, layer.b_even)))
    steps.append((2, 1.0, part(layer.back, 2, layer.b_even, layer.do, False)))
    for k in range(4):
        steps.append((1, 4.0, part(layer.attend_back, False, k // 2, (k % 2 * 4, k % 2 * 4 + 4))))
    steps.append((1, 0.3, part(layer.total, 0, layer.qkv, slice(0, D))))
    steps.append((1, 0.3, part(layer.total, 1, layer.qkv, slice(2 * D, 3 * D))))
    return steps


def layer_kernel(gather, scatter, scale, names, keys, *refs):
    units = len(BLOCKS)
    own, refs = refs[:units], refs[units:]
    hidden_in, memory_in, cot_in, dec_ref, mem_ref = refs[:5]
    block_out, grad_hidden, grad_memory = refs[5:8]
    outs, refs = refs[8 : 8 + units], refs[8 + units :]
    weights, refs = refs[:units], refs[units:]
    arrays, refs = dict(zip(names, refs[: len(names)])), refs[len(names) :]
    buffers, refs = refs[: len(keys)], refs[len(keys) :]
    send_sem, recv_sem, own_sem, credit = refs
    layer = Layer(dict(arrays, weights=weights), dec_ref, mem_ref)

    place = my_place()
    loads = [
        pltpu.make_async_copy(own[unit], weights[unit].at[block_at(place, "")], own_sem.at[unit])
        for unit in range(units)
    ]
    pairs = ((hidden_in, layer.hidden), (memory_in, layer.mem), (cot_in, layer.do))
    loads += [pltpu.make_async_copy(*pair, own_sem.at[units + k]) for k, pair in enumerate(pairs)]
    for load in loads:
        load.start()
    greet(place)

    chunks = [
        Gather(place, own[unit], weights[unit], start, width, order, number, send_sem, recv_sem)
        for number, (unit, start, width, order) in enumerate(gather)
    ]
    steps = forward_steps(layer, gather)
    loaded = set()

    def load_of(number):
        if number not in loaded:
            loaded.add(number)
            loads[number].wait()

    for number, stage in schedule(len(chunks), GATHER_STAGES, LAG):
        if stage == 1:
            load_of(gather[number][0])
        chunks[number].stage(stage)
        if stage == GATHER_STAGES - 1:
            if number == 0:
                for k in range(3):
                    load_of(units + k)
            spent = 0.0
            while steps and steps[0][0] <= number and spent < FORWARD_SHARE:
                _, cost, step = steps.pop(0)
                step()
                spent += cost
    for _, _, step in steps:
        step()
    layer.last_norm()
    give_out = pltpu.make_async_copy(layer.do, block_out, own_sem.at[units])
    give_out.start()
    give_memory = pltpu.make_async_copy(layer.mem, grad_memory, own_sem.at[units + 1])
    give_hidden = pltpu.make_async_copy(layer.hidden, grad_hidden, own_sem.at[units + 2])

    rings = Rings(place, keys, buffers, credit, scatter)
    chunks = [
        Scatter(place, rings, weights[piece[0]], outs[piece[0]], scale, piece, number, send_sem, recv_sem)
        for number, piece in enumerate(scatter)
    ]
    steps = backward_steps(layer, give_out)
    rank = {unit: k for k, unit in enumerate(SCATTER_UNITS)}
    sources = {
        7: layer.b_even,
        6: layer.slope,
        5: layer.b_odd,
        4: layer.kv2,
        3: layer.q2,
        2: layer.b_even,
        1: layer.qkv,
    }
    begun = set()

    def begin(unit):
        if unit == 7:
            layer.turn_feed()
        elif unit == 0:
            layer.pack_sums()
        else:
            layer.turn({6: layer.second, 5: layer.mixed2, 4: layer.mem, 3: layer.first, 2: layer.mixed, 1: layer.hidden}[unit])
        if unit == 4:
            layer.back(4, layer.kv2, layer.mem, False)
            layer.total(4, layer.kv2, slice(D, 2 * D))
            give_memory.start()
        if unit == 1:
            layer.back(1, layer.qkv, layer.hidden, True)
            give_hidden.start()

    for number, stage in schedule(len(chunks), SCATTER_STAGES, LAG):
        if stage == 0:
            unit = scatter[number][0]
            while steps and rank[steps[0][0]] <= rank[unit]:
                steps.pop(0)[2]()
            if unit not in begun:
                begun.add(unit)
                begin(unit)
            if unit:
                layer.outer(unit, sources[unit], scatter[number])
        chunks[number].stage(stage)
        if stage == 0:
            spent = 0.0
            while steps and spent < BACKWARD_SHARE and (steps[0][0] != 3 or rank[unit] > 0):
                _, cost, step = steps.pop(0)
                step()
                spent += cost
    give_memory.wait()
    give_hidden.wait()


def ordered(plan, order):
    return [piece for unit in order for piece in plan if piece[0] == unit]


def layer_call(hidden_in, memory, dec_lengths, mem_lengths, cotangent, owned, scale):
    units = len(BLOCKS)
    gather = gather_plan(GATHER_UNITS, 32 * WIDTH)
    scatter = scatter_plan(SCATTER_UNITS, WIDTH)
    keys = ring_keys()
    arrays = {
        "vec": ((16, D), F32),
        "feed": ((8, FF), F32),
        "sums": ((16, D), F32),
        "feed_sum": ((8, FF), F32),
        "hidden": ((ROWS, D), BF16),
        "mem": ((KEYS, D), BF16),
        "qkv": ((ROWS, 3 * D), BF16),
        "mixed": ((ROWS, D), BF16),
        "xhat": ((2, ROWS, D), BF16),
        "inv": ((2, ROWS, 128), F32),
        "first": ((ROWS, D), BF16),
        "q2": ((ROWS, D), BF16),
        "kv2": ((KEYS, 2 * D), BF16),
        "mixed2": ((ROWS, D), BF16),
        "second": ((ROWS, D), BF16),
        "act": ((ROWS, FF), BF16),
        "slope": ((ROWS, FF), BF16),
        "turned_feed": ((32, 128, 256), BF16),
        "g": ((ROWS, D), F32),
        "acc": ((ROWS, D), F32),
        "b_even": ((ROWS, D), BF16),
        "b_odd": ((ROWS, D), BF16),
        "do": ((ROWS, D), BF16),
    }
    any_spec = pl.BlockSpec(memory_space=pl.ANY)
    vmem = pl.BlockSpec(memory_space=pltpu.VMEM)
    smem = pl.BlockSpec(memory_space=pltpu.SMEM)
    dma = pltpu.SemaphoreType.DMA
    return pl.pallas_call(
        functools.partial(layer_kernel, gather, scatter, scale, tuple(arrays), keys),
        out_shape=[jax.ShapeDtypeStruct(a.shape, BF16) for a in (hidden_in, hidden_in, memory)]
        + [jax.ShapeDtypeStruct(block, F32) for block in BLOCKS],
        in_specs=[any_spec] * (units + 3) + [smem] * 2,
        out_specs=[any_spec] * 3 + [vmem] * units,
        scratch_shapes=[pltpu.VMEM((4, 2, 2, 2, *block), BF16) for block in BLOCKS]
        + [pltpu.VMEM(*array) for array in arrays.values()]
        + [pltpu.VMEM(ring_shape(key, WIDTH), BF16) for key in keys]
        + [dma((WINDOW, 6))] * 2
        + [dma((units + 3,)), pltpu.SemaphoreType.REGULAR((len(keys), 4))],
        compiler_params=pltpu.CompilerParams(collective_id=0, has_side_effects=True, vmem_limit_bytes=VMEM_LIMIT),
        name="decoder_layer",
    )(*owned, hidden_in, memory, cotangent, dec_lengths, mem_lengths)


def gelu_tanh(value):
    inner = gelu_coef * (value + 0.044715 * value * value * value)
    return 0.5 * value * (1.0 + jnp.tanh(inner))


def gelu_slope(value):
    inner = gelu_coef * (value + 0.044715 * value * value * value)
    tangent = jnp.tanh(inner)
    return 0.5 * (1.0 + tangent) + 0.5 * value * (1.0 - tangent * tangent) * gelu_coef * (
        1.0 + 3.0 * 0.044715 * value * value
    )


def product(rows_mat, weight):
    return jnp.dot(rows_mat, weight, preferred_element_type=F32)


def times_trans(rows_mat, weight):
    return jnp.einsum("tj,ij->ti", rows_mat, weight, preferred_element_type=F32)


def outer_sum(left_rows, right_rows):
    return jnp.einsum("ti,tj->ij", left_rows, right_rows, preferred_element_type=F32)


def column_total(rows_mat):
    return jnp.sum(rows_mat.astype(F32), 0)


def layer_norm(resid, gain, shift):
    center = resid - jnp.mean(resid, -1, keepdims=True)
    inv_dev = lax.rsqrt(jnp.mean(center * center, -1, keepdims=True) + epsilon)
    scaled = center * inv_dev
    return (scaled * gain + shift, scaled, inv_dev)


def norm_back(grad_out, scaled, inv_dev, gain):
    grad_scaled = grad_out * gain
    grad_resid = inv_dev * (
        grad_scaled
        - jnp.mean(grad_scaled, -1, keepdims=True)
        - scaled * jnp.mean(grad_scaled * scaled, -1, keepdims=True)
    )
    return (grad_resid, jnp.sum(grad_out * scaled, 0), jnp.sum(grad_out, 0))


def split_heads(matrix, length):
    return matrix.reshape(-1, length, HEADS, HEAD_DIM)


def merge_heads(tensor):
    return tensor.reshape(-1, D)


def scores_of(query_rows, key_rows, allowed):
    keys = allowed.shape[-1]
    raw = jnp.einsum(
        "sqhe,skhe->shqk",
        split_heads(query_rows, DEC),
        split_heads(key_rows, keys),
        preferred_element_type=F32,
    )
    return jnp.where(allowed[:, None], raw * HEAD_DIM ** (-0.5), -1000000000.0)


def attend(query_rows, key_rows, value_rows, allowed):
    scores = scores_of(query_rows, key_rows, allowed)
    top_score = jnp.max(scores, -1, keepdims=True)
    log_total = top_score + jnp.log(jnp.sum(jnp.exp(scores - top_score), -1, keepdims=True))
    probabilities = jnp.exp(scores - log_total).astype(BF16)
    mixed = jnp.einsum(
        "shqk,skhe->sqhe",
        probabilities,
        split_heads(value_rows, allowed.shape[-1]),
        preferred_element_type=F32,
    )
    return (merge_heads(mixed).astype(BF16), log_total)


def attend_back(query_rows, key_rows, value_rows, allowed, log_total, grad_mixed):
    keys = allowed.shape[-1]
    probabilities = jnp.exp(scores_of(query_rows, key_rows, allowed) - log_total)
    grad_heads = split_heads(grad_mixed, DEC)
    grad_value = jnp.einsum(
        "shqk,sqhe->skhe", probabilities.astype(BF16), grad_heads, preferred_element_type=F32
    )
    grad_probs = jnp.einsum(
        "sqhe,skhe->shqk", grad_heads, split_heads(value_rows, keys), preferred_element_type=F32
    )
    grad_scores = probabilities * (
        grad_probs - jnp.sum(probabilities * grad_probs, -1, keepdims=True)
    )
    grad_raw = (grad_scores * HEAD_DIM ** (-0.5)).astype(BF16)
    grad_query = jnp.einsum(
        "shqk,skhe->sqhe", grad_raw, split_heads(key_rows, keys), preferred_element_type=F32
    )
    grad_key = jnp.einsum(
        "shqk,sqhe->skhe", grad_raw, split_heads(query_rows, DEC), preferred_element_type=F32
    )
    return (
        merge_heads(grad_query).astype(BF16),
        merge_heads(grad_key).astype(BF16),
        merge_heads(grad_value).astype(BF16),
    )


def masks_for(dec_lengths, mem_lengths):
    row_ids = jnp.arange(DEC)
    inside = row_ids[None, :] < dec_lengths[:, None]
    valid_rows = inside.reshape(-1, 1)
    causal = (row_ids[None, None, :] <= row_ids[None, :, None]) & inside[:, None, :]
    mem_seen = (jnp.arange(MEM)[None, :] < mem_lengths[:, None])[:, None, :]
    mem_seen = jnp.broadcast_to(mem_seen, (mem_lengths.shape[0], DEC, MEM))
    return (valid_rows, causal, mem_seen)


def run_forward(weights, hidden, mem_rows, dec_lengths, mem_lengths):
    (
        self_project,
        self_output,
        cross_query,
        cross_memory,
        cross_output,
        feed_in,
        feed_out,
        bias_rows,
        feed_bias,
        norm_gains,
        norm_shifts,
    ) = weights
    bias_full = bias_rows.astype(F32)
    gain_full = norm_gains.astype(F32)
    shift_full = norm_shifts.astype(F32)
    valid_rows, causal, mem_seen = masks_for(dec_lengths, mem_lengths)
    projected = product(hidden, self_project)
    query_rows = (projected[:, :D] + bias_full[0]).astype(BF16)
    key_rows = projected[:, D : 2 * D].astype(BF16)
    value_rows = (projected[:, 2 * D :] + bias_full[1]).astype(BF16)
    mixed, log_one = attend(query_rows, key_rows, value_rows, causal)
    resid_one = alpha_res * hidden.astype(F32) + product(mixed, self_output) + bias_full[2]
    first, scaled_one, inv_one = layer_norm(resid_one, gain_full[0], shift_full[0])
    first = first.astype(BF16)
    cross_q = (product(first, cross_query) + bias_full[3]).astype(BF16)
    mem_proj = product(mem_rows, cross_memory)
    cross_k = mem_proj[:, :D].astype(BF16)
    cross_v = (mem_proj[:, D:] + bias_full[4]).astype(BF16)
    mixed_two, log_two = attend(cross_q, cross_k, cross_v, mem_seen)
    resid_two = (
        alpha_res * first.astype(F32) + product(mixed_two, cross_output) + bias_full[5]
    )
    second, scaled_two, inv_two = layer_norm(resid_two, gain_full[1], shift_full[1])
    second = second.astype(BF16)
    pre_act = product(second, feed_in) + feed_bias.astype(F32)
    active = gelu_tanh(pre_act).astype(BF16)
    resid_three = alpha_res * second.astype(F32) + product(active, feed_out) + bias_full[6]
    normed, scaled_three, inv_three = layer_norm(resid_three, gain_full[2], shift_full[2])
    block_out = jnp.where(valid_rows, normed, 0.0).astype(BF16)
    saved = (
        query_rows,
        key_rows,
        value_rows,
        log_one,
        mixed,
        scaled_one,
        inv_one,
        first,
        cross_q,
        cross_k,
        cross_v,
        log_two,
        mixed_two,
        scaled_two,
        inv_two,
        second,
        pre_act,
        active,
        scaled_three,
        inv_three,
    )
    return (saved, block_out)


def run_backward(weights, saved, hidden, mem_rows, cot_rows, dec_lengths, mem_lengths):
    (
        self_project,
        self_output,
        cross_query,
        cross_memory,
        cross_output,
        feed_in,
        feed_out,
        bias_rows,
        feed_bias,
        norm_gains,
        norm_shifts,
    ) = weights
    (
        query_rows,
        key_rows,
        value_rows,
        log_one,
        mixed,
        scaled_one,
        inv_one,
        first,
        cross_q,
        cross_k,
        cross_v,
        log_two,
        mixed_two,
        scaled_two,
        inv_two,
        second,
        pre_act,
        active,
        scaled_three,
        inv_three,
    ) = saved
    gain_full = norm_gains.astype(F32)
    valid_rows, causal, mem_seen = masks_for(dec_lengths, mem_lengths)
    grad_top = jnp.where(valid_rows, cot_rows.astype(F32), 0.0)
    grad_three, gain_three, shift_three = norm_back(grad_top, scaled_three, inv_three, gain_full[2])
    branch_three = grad_three.astype(BF16)
    grad_feed_out = outer_sum(active, branch_three)
    grad_pre = (times_trans(branch_three, feed_out) * gelu_slope(pre_act)).astype(BF16)
    grad_feed_in = outer_sum(second, grad_pre)
    grad_second = (alpha_res * grad_three + times_trans(grad_pre, feed_in)).astype(BF16)
    grad_two, gain_two, shift_two = norm_back(
        grad_second.astype(F32), scaled_two, inv_two, gain_full[1]
    )
    branch_two = grad_two.astype(BF16)
    grad_cross_output = outer_sum(mixed_two, branch_two)
    grad_mixed_two = times_trans(branch_two, cross_output).astype(BF16)
    grad_cq, grad_ck, grad_cv = attend_back(
        cross_q, cross_k, cross_v, mem_seen, log_two, grad_mixed_two
    )
    grad_mem_proj = jnp.concatenate([grad_ck, grad_cv], 1)
    grad_cross_memory = outer_sum(mem_rows, grad_mem_proj)
    grad_mem_rows = times_trans(grad_mem_proj, cross_memory).astype(BF16)
    grad_cross_query = outer_sum(first, grad_cq)
    grad_first = (alpha_res * grad_two + times_trans(grad_cq, cross_query)).astype(BF16)
    grad_one, gain_one, shift_one = norm_back(
        grad_first.astype(F32), scaled_one, inv_one, gain_full[0]
    )
    branch_one = grad_one.astype(BF16)
    grad_self_output = outer_sum(mixed, branch_one)
    grad_mixed = times_trans(branch_one, self_output).astype(BF16)
    grad_q, grad_k, grad_v = attend_back(
        query_rows, key_rows, value_rows, causal, log_one, grad_mixed
    )
    grad_projected = jnp.concatenate([grad_q, grad_k, grad_v], 1)
    grad_self_project = outer_sum(hidden, grad_projected)
    grad_hidden = (alpha_res * grad_one + times_trans(grad_projected, self_project)).astype(
        BF16
    )
    grad_bias_rows = jnp.stack(
        [
            column_total(grad_q),
            column_total(grad_v),
            column_total(branch_one),
            column_total(grad_cq),
            column_total(grad_cv),
            column_total(branch_two),
            column_total(branch_three),
        ]
    )
    grads = (
        grad_self_project,
        grad_self_output,
        grad_cross_query,
        grad_cross_memory,
        grad_cross_output,
        grad_feed_in,
        grad_feed_out,
        grad_bias_rows,
        column_total(grad_pre),
        jnp.stack([gain_one, gain_two, gain_three]),
        jnp.stack([shift_one, shift_two, shift_three]),
    )
    return (grads, grad_hidden, grad_mem_rows)


SMALL = 13


def pack_small(bias_rows, feed_bias, norm_gains, norm_shifts):
    rows = jnp.concatenate([bias_rows, norm_gains, norm_shifts], 0)
    span = rows.shape[1]
    lane = lax.broadcasted_iota(jnp.int32, (SMALL, 128), 1) // span
    rows = jnp.where(lane == lax.axis_index("shard"), jnp.tile(rows, (1, 128 // span)), 0)
    rest = jnp.zeros((2, 128), BF16)
    return jnp.concatenate([rows, feed_bias[None], rest], 0)


def hand_out_kernel(count, *refs):
    small, large, refs = refs[0], refs[1 : 1 + count], refs[1 + count :]
    bias, feed, gains, shifts = refs[:4]
    outs, held, sem = refs[4 : 4 + count], refs[4 + count : 4 + 2 * count], refs[-1]
    reads = [pltpu.make_async_copy(large[k], held[k], sem.at[0, k]) for k in range(count)]
    writes = [pltpu.make_async_copy(held[k], outs[k], sem.at[1, k]) for k in range(count)]
    for copy in reads:
        copy.start()
    shard = lax.axis_index("shard")
    mine = jnp.zeros((16, 32), F32)
    for k in range(4):
        mine += jnp.where(shard == k, small[:, k * 32 : k * 32 + 32], 0.0)
    bias[...] = mine[:7]
    gains[...] = mine[7:10]
    shifts[...] = mine[10:SMALL]
    feed[...] = small[SMALL : SMALL + 1]
    for read, write in zip(reads, writes):
        read.wait()
        write.start()
    for copy in writes:
        copy.wait()


def hand_out(small, large):
    any_spec = pl.BlockSpec(memory_space=pl.ANY)
    vmem = pl.BlockSpec(memory_space=pltpu.VMEM)
    count = len(large)
    vectors = [jax.ShapeDtypeStruct(shape, F32) for shape in ((7, 32), (1, 128), (3, 32), (3, 32))]
    bias, feed, gains, shifts, *rest = pl.pallas_call(
        functools.partial(hand_out_kernel, count),
        out_shape=vectors + [jax.ShapeDtypeStruct(a.shape, a.dtype) for a in large],
        in_specs=[vmem] + [any_spec] * count,
        out_specs=[vmem] * 4 + [any_spec] * count,
        scratch_shapes=[pltpu.VMEM(a.shape, a.dtype) for a in large] + [pltpu.SemaphoreType.DMA((2, count))],
        compiler_params=pltpu.CompilerParams(vmem_limit_bytes=VMEM_LIMIT),
        name="hand_out",
    )(small, *large)
    return (*rest, bias, feed[0], gains, shifts)


def gather_by_collectives(owned):
    axis = [0] * 7 + [1, 0, 1, 1]
    return tuple(lax.all_gather(a, AXES, axis=d, tiled=True) for a, d in zip(owned, axis))


def scatter_by_collectives(grads, factor):
    axis = [0] * 7 + [1, 0, 1, 1]
    return tuple(
        lax.psum_scatter(a * factor, AXES, scatter_dimension=d, tiled=True) for a, d in zip(grads, axis)
    )


def body(by_kernel, hidden_in, memory, dec_lengths, mem_lengths, cotangent, *owned):
    token_count = hidden_in.shape[0] * lax.axis_size(AXES)
    factor = float(token_count) ** (-0.5)
    if by_kernel:
        packed = (pack_small(*owned[7:]), *owned[:7])
        block_out, grad_hidden, grad_memory, *shares = layer_call(
            hidden_in, memory, dec_lengths, mem_lengths, cotangent, packed, factor
        )
        return hand_out(shares[0], (block_out, grad_hidden, grad_memory, *shares[1:]))
    weights = gather_by_collectives(owned)
    saved, block_out = run_forward(weights, hidden_in, memory, dec_lengths, mem_lengths)
    grads, grad_hidden, grad_memory = run_backward(
        weights, saved, hidden_in, memory, cotangent, dec_lengths, mem_lengths
    )
    return (block_out, grad_hidden, grad_memory, *scatter_by_collectives(grads, factor))


def solution(mesh):
    rows, columns, vector = P(AXES, None), P(None, AXES), P(AXES)
    in_specs = (rows, rows, vector, vector, rows, *[rows] * 7, columns, vector, columns, columns)
    out_specs = (rows, rows, rows, *[rows] * 7, columns, vector, columns, columns)
    by_kernel = mesh.shape["dp"] == 8 and mesh.shape["shard"] == 4
    return jax.shard_map(
        functools.partial(body, by_kernel), mesh=mesh, in_specs=in_specs, out_specs=out_specs, check_vma=False
    )
```

```python
import functools
import math

import jax
import jax.numpy as jnp
from jax import lax
from jax.experimental import pallas as pl
from jax.experimental.pallas import tpu as pltpu
from jax.sharding import PartitionSpec as P

D = 1024
HEADS = 16
HEAD_DIM = 64
DEC = 128
MEM = 256
AXES = ("dp", "shard")
MESH_ID = pl.DeviceIdType.MESH
BF16 = jnp.bfloat16
F32 = jnp.float32

alpha_res = 300.0**0.25
epsilon = 1e-05
gelu_coef = math.sqrt(2.0 / math.pi)

SIZES = {"z": 4, "x": 2, "y": 2}
FF = 4096
LAG = 4
WINDOW = 32
SLOTS = {"s": 5}
FORWARD_SHARE = 4.0
BACKWARD_SHARE = 1.0
ABREAST = 2
SPACING = 1
VMEM_LIMIT = 63 * 2**20
WIDTH = 512
GATHER_ORDERS = ("zxy", "xzy", "zyx", "yzx", "xzy", "yzx")
SCATTER_ORDERS = ("yxz", "yzx", "xyz", "xzy", "yzx", "xzy")


def my_place():
    dp, shard = lax.axis_index("dp"), lax.axis_index("shard")
    place = {
        "z": lax.div(dp, 2),
        "x": lax.rem(dp, 2),
        "y": lax.div(shard, 2),
        "c": lax.rem(shard, 2),
    }
    z = place["z"]
    place["middle"] = (z == 1) | (z == 2)
    place["end"] = (z == 0) | (z == 3)
    place["pair"] = z + 1 - 2 * lax.rem(z, 2)
    place["far"] = 2 - 2 * lax.div(z, 2)
    place["across"] = 2 - lax.div(z, 2)
    place["beyond"] = 3 - 3 * lax.div(z, 2)
    return place


def device_of(place):
    return (place["z"] * 2 + place["x"], place["y"] * 2 + place["c"])


def moved(place, **changes):
    return {**place, **changes}


def across(place, dim):
    key = "c" if dim == "s" else dim
    return moved(place, **{key: 1 - place[key]})


def greet(place):
    barrier = pltpu.get_barrier_semaphore()
    others = [across(place, dim) for dim in "xys"]
    others += [moved(place, z=lax.rem(place["z"] + k, 4)) for k in (1, 2, 3)]
    for other in others:
        pl.semaphore_signal(barrier, inc=1, device_id=device_of(other), device_id_type=MESH_ID)
    pl.semaphore_wait(barrier, len(others))


def block_at(place, whole):
    return tuple(pl.ds(0, SIZES.get(d, 2)) if d in whole else place[d] for d in ("z", "x", "y", "c"))


def when(condition, action):
    if condition is True:
        action()
    else:
        pl.when(condition)(action)


class Mover:
    def __init__(self, place, number, send_sem, recv_sem):
        self.place, self.number = place, number % WINDOW
        self.send_sem, self.recv_sem = send_sem, recv_sem
        self.waiting = []

    def move(self, source, target, slot, other, sends=True, receives=True):
        copy = pltpu.make_async_remote_copy(
            src_ref=source,
            dst_ref=target,
            send_sem=self.send_sem.at[self.number, slot],
            recv_sem=self.recv_sem.at[self.number, slot],
            device_id=device_of(other),
            device_id_type=MESH_ID,
        )
        when(sends, copy.start)
        self.waiting.append((copy, sends, receives))

    def settle(self):
        for copy, sends, receives in self.waiting:
            when(receives, copy.wait_recv)
            when(sends, copy.wait_send)
        self.waiting = []


SLOT = {"x": 0, "y": 1, "s": 2}


class Gather(Mover):
    def __init__(self, place, own, full, start, width, order, number, send_sem, recv_sem):
        super().__init__(place, number, send_sem, recv_sem)
        self.own, self.full = own, full
        self.columns = pl.ds(start, width)
        self.path, held = [], ""
        for dim in order + "s":
            self.path += [(step, held) for step in (("near", "on") if dim == "z" else dim)]
            held += dim

    def part(self, index):
        return self.full.at[(*index, slice(None), self.columns)]

    def stage(self, number):
        self.settle()
        if number == GATHER_STAGES - 1:
            return
        dim, held = self.path[number]
        place = self.place
        index = block_at(place, held)
        target = self.part(index)
        source = target if number else self.own.at[:, self.columns]
        if dim == "near":
            self.move(source, target, 3, moved(place, z=place["pair"]))
            for slot, sends in ((4, place["end"]), (5, place["middle"])):
                self.move(source, target, slot, moved(place, z=place["across"]), sends, place["middle"])
        elif dim == "on":
            both = self.part((pl.ds(place["far"], 2), *index[1:]))
            self.move(both, both, 4, moved(place, z=place["pair"]), place["middle"], place["end"])
        else:
            self.move(source, target, SLOT[dim], across(place, dim))


GATHER_STAGES = 6
SCATTER_STAGES = 6


def schedule(count, stages, lag):
    for step in range(count + (stages - 1) * lag):
        for stage in reversed(range(stages)):
            if 0 <= step - stage * lag < count:
                yield step - stage * lag, stage


def gather_plan(units, size):
    plan = []
    for unit in units:
        rows, columns = BLOCKS[unit]
        width = min(columns, max(128, size // rows))
        for start in range(0, columns, width):
            plan.append((unit, start, width, GATHER_ORDERS[len(plan) % len(GATHER_ORDERS)]))
    return plan


def rings_of(order):
    keys = [("s", "zxy")]
    left = "zxy"
    for dim in order:
        left = left.replace(dim, "")
        keys += [("fold", left), ("share", left)] if dim == "z" else [(dim, left)]
    return keys


def slots_of(key):
    return SLOTS.get(key[0], 3)


def ring_shape(key, width):
    step, left = key
    return (slots_of(key), 2 if step in ("fold", "share") else 1, *[SIZES[d] for d in left], 32, width)


class Rings:
    def __init__(self, place, keys, buffers, credit, plan):
        self.place, self.credit = place, credit
        self.number = {key: k for k, key in enumerate(keys)}
        self.buffer = dict(zip(keys, buffers))
        users = {key: [] for key in keys}
        for number, piece in enumerate(plan):
            for key in rings_of(piece[5]):
                users[key].append(number)
        for key, numbers in users.items():
            slots = slots_of(key)
            assert all(b - a >= LAG for a, b in zip(numbers, numbers[slots:]))
        self.uses = {key: len(numbers) for key, numbers in users.items()}
        self.turn = {key: 0 for key in keys}

    def links(self, key):
        step, place = key[0], self.place
        pair = moved(place, z=place["pair"])
        if step == "fold":
            return [(0, place["end"], pair, place["middle"])]
        if step == "share":
            other = moved(place, z=place["across"])
            return [
                (1, True, pair, True),
                (2, place["middle"], other, place["middle"]),
                (3, place["middle"], other, place["end"]),
            ]
        return [(0, True, across(place, step), True)]

    def take(self, key):
        turn = self.turn[key]
        self.turn[key] += 1
        if turn >= slots_of(key):
            for slot, sends, _, _ in self.links(key):
                when(sends, functools.partial(pl.semaphore_wait, self.credit.at[self.number[key], slot], 1))
        return turn % slots_of(key)

    def give(self, key):
        self.given = getattr(self, "given", {})
        turn = self.given[key] = self.given.get(key, -1) + 1
        if turn + slots_of(key) >= self.uses[key]:
            return
        for slot, _, other, receives in self.links(key):
            when(
                receives,
                functools.partial(
                    pl.semaphore_signal,
                    self.credit.at[self.number[key], slot],
                    inc=1,
                    device_id=device_of(other),
                    device_id_type=MESH_ID,
                ),
            )


class Scatter(Mover):
    def __init__(self, place, rings, grads, out, scale, piece, number, send_sem, recv_sem):
        super().__init__(place, number, send_sem, recv_sem)
        _, row, rows, start, width, order = piece
        self.rings, self.grads, self.out, self.scale = rings, grads, out, scale
        self.part = (pl.ds(row, rows), pl.ds(start, width))
        self.corner = (pl.ds(0, rows), pl.ds(0, width))
        self.keys = rings_of(order)

    def send(self, stage):
        key = self.keys[stage]
        step, left = key
        place = self.place
        self.slot = self.rings.take(key)
        buffer = self.rings.buffer[key]
        inner = [slice(None)] * len(left)

        def mine(place):
            return self.grads.at[(*block_at(place, left), *self.part)]

        if step == "fold":
            index = block_at(place, left)
            source = self.grads.at[(pl.ds(place["far"], 2), *index[1:], *self.part)]
            target = buffer.at[(self.slot, slice(None), *inner, *self.corner)]
            self.move(source, target, 5, moved(place, z=place["pair"]), place["end"], place["middle"])
        elif step == "share":
            targets = [buffer.at[(self.slot, k, *inner, *self.corner)] for k in (0, 1)]
            pair, middle, end = (moved(place, z=place[d]) for d in ("pair", "across", "beyond"))
            self.move(mine(pair), targets[0], 3, pair)
            self.move(mine(middle), targets[1], 4, middle, place["middle"], place["middle"])
            self.move(mine(end), targets[1], 5, end, place["middle"], place["end"])
        else:
            other = across(place, step)
            self.move(mine(other), buffer.at[(self.slot, 0, *inner, *self.corner)], SLOT[step], other)

    def add(self, stage):
        key = self.keys[stage]
        step, left = key
        place = self.place
        self.settle()
        buffer = self.rings.buffer[key]

        def fold(index, inner, count=1, first=0):
            value = self.grads[(*index, *self.part)].astype(F32)
            for k in range(first, first + count):
                value += buffer[(self.slot, k, *inner, *self.corner)].astype(F32)
            return value

        def add_all():
            if step == "fold":
                for k in (0, 1):
                    index = block_at(moved(place, z=place["far"] + k), left)
                    inner = (slice(None),) * len(left)
                    self.grads[(*index, *self.part)] = fold(index, inner, 1, k).astype(BF16)
                return
            count = 2 if step == "share" else 1
            if not left:
                self.out[self.part] = fold(block_at(place, left), (), count) * self.scale
                return
            first, rest = left[0], left[1:]

            def body(i, _):
                index = block_at(moved(place, **{first: i}), rest)
                inner = (i, *[slice(None)] * len(rest))
                self.grads[(*index, *self.part)] = fold(index, inner, count).astype(BF16)
                return 0

            lax.fori_loop(0, SIZES[first], body, 0)

        when(place["middle"] if step == "fold" else True, add_all)
        self.rings.give(key)

    def stage(self, number):
        if number > 0:
            self.add(number - 1)
        if number < SCATTER_STAGES - 1:
            self.send(number)


def scatter_plan(units, width):
    plan = []
    for unit in units:
        rows, columns = BLOCKS[unit]
        for row in range(0, rows, 32):
            for start in range(0, columns, width):
                order = SCATTER_ORDERS[len(plan) % len(SCATTER_ORDERS)]
                plan.append((unit, row, min(rows, 32), start, min(columns, width), order))
    return plan


def ring_keys():
    return sorted({key for order in SCATTER_ORDERS for key in rings_of(order)})


BLOCKS = ((16, 128), (32, 3 * D), (32, D), (32, D), (32, 2 * D), (32, D), (32, FF), (128, D))
GATHER_UNITS = (0, 1, 4, 2, 3, 5, 6, 7)
SCATTER_UNITS = (7, 6, 5, 4, 3, 2, 0, 1)
ROWS = 2 * DEC
KEYS = 2 * MEM


def dot(left, right):
    return jnp.dot(left, right, preferred_element_type=F32)


def dot_rows(left, right):
    return lax.dot_general(left, right, (((1,), (1,)), ((), ())), preferred_element_type=F32)


def dot_columns(left, right):
    return lax.dot_general(left, right, (((0,), (0,)), ((), ())), preferred_element_type=F32)


def flat(value):
    return value.reshape(-1, value.shape[-1])


def tile(index, size):
    return pl.ds(pl.multiple_of(index * size, size), size)


def loop(count, body):
    def step(i, carry):
        body(i)
        return carry

    lax.fori_loop(0, count, step, 0)


class Layer:
    def __init__(self, refs, dec_ref, mem_ref):
        self.dec_ref, self.mem_ref = dec_ref, mem_ref
        self.__dict__.update(refs)

    def unpack(self):
        small = self.weights[0]
        for group in range(8):
            block = small[group // 2, group % 2].astype(F32)
            self.vec[:, group * 128 : (group + 1) * 128] = block[0, 0] + block[0, 1] + block[1, 0] + block[1, 1]
            for k in range(4):
                first = (group * 4 + k) * 128
                self.feed[0:1, first : first + 128] = block[k // 2, k % 2, 13:14]
        self.sums[...] = jnp.zeros_like(self.sums)

    def row(self, number, columns=slice(None)):
        return self.vec[number : number + 1, columns]

    def project(self, start, width):
        out = dot(self.hidden[...], flat(self.weights[1][..., start : start + width]))
        if start < D:
            out += self.row(0, slice(start, start + width))
        elif start >= 2 * D:
            out += self.row(1, slice(start - 2 * D, start - 2 * D + width))
        self.qkv[:, start : start + width] = out.astype(BF16)

    def project_memory(self, start, width):
        weight = flat(self.weights[4][..., start : start + width])

        def half(i):
            out = dot(self.mem[tile(i, 256), :], weight)
            if start >= D:
                out += self.row(4, slice(start - D, start - D + width))
            self.kv2[tile(i, 256), start : start + width] = out.astype(BF16)

        loop(2, half)

    def output(self, unit, source, resid, bias, start, width):
        columns = slice(start, start + width)
        out = dot(source[...], flat(self.weights[unit][..., columns])) + self.row(bias, columns)
        self.acc[:, columns] = out + alpha_res * resid[:, columns].astype(F32)

    def query(self, start, width):
        columns = slice(start, start + width)
        out = dot(self.first[...], flat(self.weights[3][..., columns])) + self.row(3, columns)
        self.q2[:, columns] = out.astype(BF16)

    def feed_up(self, start, width):
        columns = slice(start, start + width)
        pre = dot(self.second[...], flat(self.weights[6][..., columns])) + self.feed[0:1, columns]
        square = pre * pre
        tangent = jnp.tanh(gelu_coef * pre * (1.0 + 0.044715 * square))
        self.act[:, columns] = (0.5 * pre * (1.0 + tangent)).astype(BF16)
        slope = 0.5 * (1.0 + tangent) + 0.5 * pre * (1.0 - tangent * tangent) * gelu_coef * (
            1.0 + 3.0 * 0.044715 * square
        )
        self.slope[:, columns] = slope.astype(BF16)

    def standard(self, rows):
        resid = self.acc[rows, :]
        center = resid - jnp.mean(resid, -1, keepdims=True)
        inv = lax.rsqrt(jnp.mean(center * center, -1, keepdims=True) + epsilon)
        return center * inv, inv

    def norm(self, number, out):
        def some(i):
            rows = tile(i, 64)
            scaled, inv = self.standard(rows)
            self.xhat[number, rows, :] = scaled.astype(BF16)
            self.inv[number, rows, :] = jnp.broadcast_to(inv, (64, 128))
            out[rows, :] = (scaled * self.row(7 + number) + self.row(10 + number)).astype(BF16)

        loop(4, some)

    def norm_grad(self, number, grad, scaled, inv, rows, b_ref):
        grad_scaled = grad * self.row(7 + number)
        resid = inv * (
            grad_scaled
            - jnp.mean(grad_scaled, -1, keepdims=True)
            - scaled * jnp.mean(grad_scaled * scaled, -1, keepdims=True)
        )
        branch = resid.astype(BF16)
        self.g[rows, :] = resid
        b_ref[rows, :] = branch
        bias = (2, 5, 6)[number]
        self.sums[7 + number : 8 + number, :] += jnp.sum(grad * scaled, 0, keepdims=True)
        self.sums[10 + number : 11 + number, :] += jnp.sum(grad, 0, keepdims=True)
        self.sums[bias : bias + 1, :] += jnp.sum(branch.astype(F32), 0, keepdims=True)

    def last_norm(self):
        def some(i):
            rows = tile(i, 64)
            scaled, inv = self.standard(rows)
            ids = lax.broadcasted_iota(jnp.int32, (64, 1), 0) + lax.rem(i, 2) * 64
            valid = ids < self.dec_ref[lax.div(i, 2)]
            grad = jnp.where(valid, self.do[rows, :].astype(F32), 0.0)
            out = scaled * self.row(9) + self.row(12)
            self.do[rows, :] = jnp.where(valid, out, 0.0).astype(BF16)
            self.norm_grad(2, grad, scaled, inv, rows, self.b_even)

        loop(4, some)

    def norm_back(self, number, b_ref):
        def some(i):
            rows = tile(i, 64)
            grad = self.acc[rows, :].astype(BF16).astype(F32)
            scaled = self.xhat[number, rows, :].astype(F32)
            self.norm_grad(number, grad, scaled, self.inv[number, rows, 0:1], rows, b_ref)

        loop(4, some)

    def stacked(self, value):
        low = lax.broadcasted_iota(jnp.int32, (DEC, 128), 1) < HEAD_DIM
        zero = jnp.zeros_like(value)
        return jnp.concatenate([jnp.where(low, value, zero), jnp.where(low, zero, value)], 0)

    def unstacked(self, value):
        low = lax.broadcasted_iota(jnp.int32, (DEC, 128), 1) < HEAD_DIM
        return jnp.where(low, value[:DEC], value[DEC:])

    def heads(self, cross, seq, pair):
        rows = tile(seq, DEC)
        if cross:
            keys, ref, first = tile(seq, MEM), self.kv2, 0
            q_at = (self.q2, rows, tile(pair, 128))
        else:
            keys, ref, first = rows, self.qkv, 8
            q_at = (self.qkv, rows, tile(pair, 128))
        k_at = (ref, keys, tile(first + pair, 128))
        v_at = (ref, keys, tile(first + 8 + pair, 128))
        return rows, q_at, k_at, v_at

    def weights_of(self, cross, seq, queries, key_rows):
        raw = dot_rows(queries, key_rows)
        column = lax.broadcasted_iota(jnp.int32, raw.shape, 1)
        if cross:
            allowed = column < self.mem_ref[seq]
        else:
            line = lax.rem(lax.broadcasted_iota(jnp.int32, raw.shape, 0), DEC)
            allowed = (column <= line) & (column < self.dec_ref[seq])
        scores = jnp.where(allowed, raw * HEAD_DIM ** (-0.5), -1000000000.0)
        expo = jnp.exp(scores - jnp.max(scores, -1, keepdims=True))
        return expo * (1.0 / jnp.sum(expo, -1, keepdims=True))

    def attend(self, cross, seq, pairs):
        out = self.mixed2 if cross else self.mixed

        def some(i):
            held = []
            for k in range(ABREAST):
                pair = i * ABREAST + k + pairs[0]
                rows, q_at, k_at, v_at = self.heads(cross, seq, pair)
                held.append((rows, pair, *[at[0][at[1:]] for at in (q_at, k_at, v_at)]))
            mixed = []
            for _, _, queries, key_rows, value_rows in held:
                probabilities = self.weights_of(cross, seq, self.stacked(queries), key_rows)
                mixed.append(self.unstacked(dot(probabilities.astype(BF16), value_rows)).astype(BF16))
            for (rows, pair, *_), value in zip(held, mixed):
                out[rows, tile(pair, 128)] = value

        loop((pairs[1] - pairs[0]) // ABREAST, some)

    def attend_back(self, cross, seq, pairs):
        def some(i):
            held = []
            for k in range(ABREAST):
                pair = i * ABREAST + k + pairs[0]
                rows, *places = self.heads(cross, seq, pair)
                values = [at[0][at[1:]] for at in places]
                held.append((places, *values, self.do[rows, tile(pair, 128)]))
            results = []
            for _, queries, key_rows, value_rows, grads in held:
                queries, grads = self.stacked(queries), self.stacked(grads)
                probabilities = self.weights_of(cross, seq, queries, key_rows)
                grad_value = dot_columns(probabilities.astype(BF16), grads)
                grad_probs = dot_rows(grads, value_rows)
                mean = jnp.sum(probabilities * grad_probs, -1, keepdims=True)
                grad_raw = (probabilities * (grad_probs - mean) * HEAD_DIM ** (-0.5)).astype(BF16)
                grad_query = self.unstacked(dot(grad_raw, key_rows))
                grad_key = dot_columns(grad_raw, queries)
                results.append([value.astype(BF16) for value in (grad_query, grad_key, grad_value)])
            for (places, *_), values in zip(held, results):
                for at, value in zip(places, values):
                    at[0][at[1:]] = value

        loop((pairs[1] - pairs[0]) // ABREAST, some)

    def feed_down_back(self, part):
        columns = slice(part * 512, part * 512 + 512)
        grad = dot_rows(self.b_even[...], flat(self.weights[7][part // 2, part % 2]))
        grad = (grad * self.slope[:, columns].astype(F32)).astype(BF16)
        self.slope[:, columns] = grad
        self.feed_sum[0:1, columns] = jnp.sum(grad.astype(F32), 0, keepdims=True)

    def back(self, unit, source, out, resid):
        def some(z):
            columns = tile(z, 256)
            value = dot_rows(source[...], flat(self.weights[unit][z]))
            if resid:
                value += alpha_res * self.g[:, columns]
            out[:, columns] = value.astype(out.dtype)

        loop(4, some)

    def total(self, number, source, columns):
        self.sums[number : number + 1, :] = jnp.sum(source[:, columns].astype(F32), 0, keepdims=True)

    def turn(self, source):
        for k in range(source.shape[0] // 256):
            for column in range(0, D, 256):
                block = source[k * 256 : (k + 1) * 256, column : column + 256]
                first = k * D + column
                self.act[:, first : first + 256] = block.T

    def turn_feed(self):
        for k in range(8):
            block = self.act[:, k * 512 : (k + 1) * 512].T
            self.turned_feed[k * 4 : (k + 1) * 4] = block.reshape(4, 128, 256)

    def outer(self, unit, source, piece):
        _, row, rows, start, width, _ = piece
        def some(k):
            columns = pl.ds(pl.multiple_of(start + k * 256, 256), 256)
            right = source[0:256, columns]
            for z in range(4):
                if unit == 7:
                    left = flat(self.turned_feed[z * 8 : z * 8 + 8, row : row + rows, :])
                    value = dot(left, right)
                else:
                    value = dot(self.act[:, z * 256 : z * 256 + 256], right)
                    if unit == 4:
                        value += dot(self.act[:, D + z * 256 : D + z * 256 + 256], source[256:512, columns])
                value = value.astype(BF16).reshape(2, 2, 2, rows, 256)
                self.weights[unit][z, :, :, :, row : row + rows, columns] = value

        loop(width // 256, some)

    def pack_sums(self):
        small = self.weights[0]
        line = lax.broadcasted_iota(jnp.int32, (16, 128), 0)
        for group in range(8):
            block = self.sums[:, group * 128 : (group + 1) * 128]
            for k in range(4):
                first = (group * 4 + k) * 128
                feed = jnp.broadcast_to(self.feed_sum[0:1, first : first + 128], (16, 128))
                small[group // 2, group % 2, k // 2, k % 2] = jnp.where(line == 13, feed, block).astype(BF16)


def forward_steps(layer, gather):
    ready = {}
    for number, (unit, start, width, _) in enumerate(gather):
        ready.setdefault(unit, []).append((number, start, width))
    steps = [(ready[0][-1][0], 0.5, layer.unpack)]
    for number, start, width in ready[1]:
        steps.append((number, 0.7, functools.partial(layer.project, start, width)))
    memory = [(n, 1.2, functools.partial(layer.project_memory, s, w)) for n, s, w in ready[4]]
    done = ready[1][-1][0]
    for k in range(4):
        steps.append((done, 3.0, functools.partial(layer.attend, False, k // 2, (k % 2 * 4, k % 2 * 4 + 4))))
        if k < len(memory):
            steps.append(memory[k])
    steps += memory[4:]
    for number, start, width in ready[2]:
        steps.append((number, 0.7, functools.partial(layer.output, 2, layer.mixed, layer.hidden, 2, start, width)))
    steps.append((0, 1.5, functools.partial(layer.norm, 0, layer.first)))
    for number, start, width in ready[3]:
        steps.append((number, 0.7, functools.partial(layer.query, start, width)))
    for k in range(8):
        steps.append((0, 3.0, functools.partial(layer.attend, True, k // 4, (k % 4 * 2, k % 4 * 2 + 2))))
    for number, start, width in ready[5]:
        steps.append((number, 0.7, functools.partial(layer.output, 5, layer.mixed2, layer.first, 5, start, width)))
    steps.append((0, 1.5, functools.partial(layer.norm, 1, layer.second)))
    for number, start, width in ready[6]:
        steps.append((number, 1.5, functools.partial(layer.feed_up, start, width)))
    last = ready[7]
    for (_, start, width), (number, _, more) in zip(last[::2], last[1::2]):
        steps.append(
            (number, 0.8, functools.partial(layer.output, 7, layer.act, layer.second, 6, start, width + more))
        )
    return steps


def backward_steps(layer, give_out):
    part = functools.partial
    steps = [(7, 0.6, part(layer.feed_down_back, k)) for k in range(8)]
    steps.append((6, 2.5, part(layer.back, 6, layer.slope, layer.acc, True)))
    steps.append((6, 1.5, part(layer.norm_back, 1, layer.b_odd)))
    steps.append((5, 0.0, give_out.wait))
    steps.append((5, 1.0, part(layer.back, 5, layer.b_odd, layer.do, False)))
    for k in range(8):
        steps.append((4, 4.0, part(layer.attend_back, True, k // 4, (k % 4 * 2, k % 4 * 2 + 2))))
    steps.append((3, 1.0, part(layer.back, 3, layer.q2, layer.acc, True)))
    steps.append((3, 0.3, part(layer.total, 3, layer.q2, slice(0, D))))
    steps.append((3, 1.5, part(layer.norm_back, 0, layer.b_even)))
    steps.append((2, 1.0, part(layer.back, 2, layer.b_even, layer.do, False)))
    for k in range(4):
        steps.append((1, 4.0, part(layer.attend_back, False, k // 2, (k % 2 * 4, k % 2 * 4 + 4))))
    steps.append((1, 0.3, part(layer.total, 0, layer.qkv, slice(0, D))))
    steps.append((1, 0.3, part(layer.total, 1, layer.qkv, slice(2 * D, 3 * D))))
    return steps


def layer_kernel(gather, scatter, scale, names, keys, *refs):
    units = len(BLOCKS)
    own, refs = refs[:units], refs[units:]
    hidden_in, memory_in, cot_in, dec_ref, mem_ref = refs[:5]
    block_out, grad_hidden, grad_memory = refs[5:8]
    outs, refs = refs[8 : 8 + units], refs[8 + units :]
    weights, refs = refs[:units], refs[units:]
    arrays, refs = dict(zip(names, refs[: len(names)])), refs[len(names) :]
    buffers, refs = refs[: len(keys)], refs[len(keys) :]
    send_sem, recv_sem, own_sem, credit = refs
    layer = Layer(dict(arrays, weights=weights), dec_ref, mem_ref)

    place = my_place()
    loads = [
        pltpu.make_async_copy(own[unit], weights[unit].at[block_at(place, "")], own_sem.at[unit])
        for unit in range(units)
    ]
    pairs = ((hidden_in, layer.hidden), (memory_in, layer.mem), (cot_in, layer.do))
    loads += [pltpu.make_async_copy(*pair, own_sem.at[units + k]) for k, pair in enumerate(pairs)]
    for load in loads:
        load.start()
    greet(place)

    chunks = [
        Gather(place, own[unit], weights[unit], start, width, order, number, send_sem, recv_sem)
        for number, (unit, start, width, order) in enumerate(gather)
    ]
    steps = forward_steps(layer, gather)
    loaded = set()

    def load_of(number):
        if number not in loaded:
            loaded.add(number)
            loads[number].wait()

    for number, stage in schedule(len(chunks), GATHER_STAGES, LAG):
        if stage == 1:
            load_of(gather[number][0])
        chunks[number].stage(stage)
        if stage == GATHER_STAGES - 1:
            if number == 0:
                for k in range(3):
                    load_of(units + k)
            spent = 0.0
            while steps and steps[0][0] <= number and spent < FORWARD_SHARE:
                _, cost, step = steps.pop(0)
                step()
                spent += cost
    for _, _, step in steps:
        step()
    layer.last_norm()
    give_out = pltpu.make_async_copy(layer.do, block_out, own_sem.at[units])
    give_out.start()
    give_memory = pltpu.make_async_copy(layer.mem, grad_memory, own_sem.at[units + 1])
    give_hidden = pltpu.make_async_copy(layer.hidden, grad_hidden, own_sem.at[units + 2])

    rings = Rings(place, keys, buffers, credit, scatter)
    chunks = [
        Scatter(place, rings, weights[piece[0]], outs[piece[0]], scale, piece, len(gather) + number, send_sem, recv_sem)
        for number, piece in enumerate(scatter)
    ]
    steps = backward_steps(layer, give_out)
    rank = {unit: k for k, unit in enumerate(SCATTER_UNITS)}
    sources = {
        7: layer.b_even,
        6: layer.slope,
        5: layer.b_odd,
        4: layer.kv2,
        3: layer.q2,
        2: layer.b_even,
        1: layer.qkv,
    }
    begun = set()

    def begin(unit):
        if unit == 7:
            layer.turn_feed()
        elif unit == 0:
            layer.pack_sums()
        else:
            layer.turn({6: layer.second, 5: layer.mixed2, 4: layer.mem, 3: layer.first, 2: layer.mixed, 1: layer.hidden}[unit])
        if unit == 4:
            layer.back(4, layer.kv2, layer.mem, False)
            layer.total(4, layer.kv2, slice(D, 2 * D))
            give_memory.start()
        if unit == 1:
            layer.back(1, layer.qkv, layer.hidden, True)
            give_hidden.start()

    for number, stage in schedule(len(chunks), SCATTER_STAGES, LAG):
        if stage == 0:
            unit = scatter[number][0]
            while steps and rank[steps[0][0]] <= rank[unit]:
                steps.pop(0)[2]()
            if unit not in begun:
                begun.add(unit)
                begin(unit)
            if unit:
                layer.outer(unit, sources[unit], scatter[number])
        chunks[number].stage(stage)
        if stage == 3 and number % SPACING == 0:
            spent = 0.0
            unit = scatter[min(number + 3 * LAG, len(scatter) - 1)][0]
            while steps and spent < BACKWARD_SHARE and (steps[0][0] != 3 or rank[unit] > 0):
                _, cost, step = steps.pop(0)
                step()
                spent += cost
    give_memory.wait()
    give_hidden.wait()


def ordered(plan, order):
    return [piece for unit in order for piece in plan if piece[0] == unit]


def layer_call(hidden_in, memory, dec_lengths, mem_lengths, cotangent, owned, scale):
    units = len(BLOCKS)
    gather = gather_plan(GATHER_UNITS, 32 * WIDTH)
    scatter = scatter_plan(SCATTER_UNITS, WIDTH)
    keys = ring_keys()
    arrays = {
        "vec": ((16, D), F32),
        "feed": ((8, FF), F32),
        "sums": ((16, D), F32),
        "feed_sum": ((8, FF), F32),
        "hidden": ((ROWS, D), BF16),
        "mem": ((KEYS, D), BF16),
        "qkv": ((ROWS, 3 * D), BF16),
        "mixed": ((ROWS, D), BF16),
        "xhat": ((2, ROWS, D), BF16),
        "inv": ((2, ROWS, 128), F32),
        "first": ((ROWS, D), BF16),
        "q2": ((ROWS, D), BF16),
        "kv2": ((KEYS, 2 * D), BF16),
        "mixed2": ((ROWS, D), BF16),
        "second": ((ROWS, D), BF16),
        "act": ((ROWS, FF), BF16),
        "slope": ((ROWS, FF), BF16),
        "turned_feed": ((32, 128, 256), BF16),
        "g": ((ROWS, D), F32),
        "acc": ((ROWS, D), F32),
        "b_even": ((ROWS, D), BF16),
        "b_odd": ((ROWS, D), BF16),
        "do": ((ROWS, D), BF16),
    }
    any_spec = pl.BlockSpec(memory_space=pl.ANY)
    vmem = pl.BlockSpec(memory_space=pltpu.VMEM)
    smem = pl.BlockSpec(memory_space=pltpu.SMEM)
    dma = pltpu.SemaphoreType.DMA
    return pl.pallas_call(
        functools.partial(layer_kernel, gather, scatter, scale, tuple(arrays), keys),
        out_shape=[jax.ShapeDtypeStruct(a.shape, BF16) for a in (hidden_in, hidden_in, memory)]
        + [jax.ShapeDtypeStruct(block, F32) for block in BLOCKS],
        in_specs=[any_spec] * (units + 3) + [smem] * 2,
        out_specs=[any_spec] * 3 + [vmem] * units,
        scratch_shapes=[pltpu.VMEM((4, 2, 2, 2, *block), BF16) for block in BLOCKS]
        + [pltpu.VMEM(*array) for array in arrays.values()]
        + [pltpu.VMEM(ring_shape(key, WIDTH), BF16) for key in keys]
        + [dma((WINDOW, 6))] * 2
        + [dma((units + 3,)), pltpu.SemaphoreType.REGULAR((len(keys), 4))],
        compiler_params=pltpu.CompilerParams(collective_id=0, has_side_effects=True, vmem_limit_bytes=VMEM_LIMIT),
        name="decoder_layer",
    )(*owned, hidden_in, memory, cotangent, dec_lengths, mem_lengths)


def gelu_tanh(value):
    inner = gelu_coef * (value + 0.044715 * value * value * value)
    return 0.5 * value * (1.0 + jnp.tanh(inner))


def gelu_slope(value):
    inner = gelu_coef * (value + 0.044715 * value * value * value)
    tangent = jnp.tanh(inner)
    return 0.5 * (1.0 + tangent) + 0.5 * value * (1.0 - tangent * tangent) * gelu_coef * (
        1.0 + 3.0 * 0.044715 * value * value
    )


def product(rows_mat, weight):
    return jnp.dot(rows_mat, weight, preferred_element_type=F32)


def times_trans(rows_mat, weight):
    return jnp.einsum("tj,ij->ti", rows_mat, weight, preferred_element_type=F32)


def outer_sum(left_rows, right_rows):
    return jnp.einsum("ti,tj->ij", left_rows, right_rows, preferred_element_type=F32)


def column_total(rows_mat):
    return jnp.sum(rows_mat.astype(F32), 0)


def layer_norm(resid, gain, shift):
    center = resid - jnp.mean(resid, -1, keepdims=True)
    inv_dev = lax.rsqrt(jnp.mean(center * center, -1, keepdims=True) + epsilon)
    scaled = center * inv_dev
    return (scaled * gain + shift, scaled, inv_dev)


def norm_back(grad_out, scaled, inv_dev, gain):
    grad_scaled = grad_out * gain
    grad_resid = inv_dev * (
        grad_scaled
        - jnp.mean(grad_scaled, -1, keepdims=True)
        - scaled * jnp.mean(grad_scaled * scaled, -1, keepdims=True)
    )
    return (grad_resid, jnp.sum(grad_out * scaled, 0), jnp.sum(grad_out, 0))


def split_heads(matrix, length):
    return matrix.reshape(-1, length, HEADS, HEAD_DIM)


def merge_heads(tensor):
    return tensor.reshape(-1, D)


def scores_of(query_rows, key_rows, allowed):
    keys = allowed.shape[-1]
    raw = jnp.einsum(
        "sqhe,skhe->shqk",
        split_heads(query_rows, DEC),
        split_heads(key_rows, keys),
        preferred_element_type=F32,
    )
    return jnp.where(allowed[:, None], raw * HEAD_DIM ** (-0.5), -1000000000.0)


def attend(query_rows, key_rows, value_rows, allowed):
    scores = scores_of(query_rows, key_rows, allowed)
    top_score = jnp.max(scores, -1, keepdims=True)
    log_total = top_score + jnp.log(jnp.sum(jnp.exp(scores - top_score), -1, keepdims=True))
    probabilities = jnp.exp(scores - log_total).astype(BF16)
    mixed = jnp.einsum(
        "shqk,skhe->sqhe",
        probabilities,
        split_heads(value_rows, allowed.shape[-1]),
        preferred_element_type=F32,
    )
    return (merge_heads(mixed).astype(BF16), log_total)


def attend_back(query_rows, key_rows, value_rows, allowed, log_total, grad_mixed):
    keys = allowed.shape[-1]
    probabilities = jnp.exp(scores_of(query_rows, key_rows, allowed) - log_total)
    grad_heads = split_heads(grad_mixed, DEC)
    grad_value = jnp.einsum(
        "shqk,sqhe->skhe", probabilities.astype(BF16), grad_heads, preferred_element_type=F32
    )
    grad_probs = jnp.einsum(
        "sqhe,skhe->shqk", grad_heads, split_heads(value_rows, keys), preferred_element_type=F32
    )
    grad_scores = probabilities * (
        grad_probs - jnp.sum(probabilities * grad_probs, -1, keepdims=True)
    )
    grad_raw = (grad_scores * HEAD_DIM ** (-0.5)).astype(BF16)
    grad_query = jnp.einsum(
        "shqk,skhe->sqhe", grad_raw, split_heads(key_rows, keys), preferred_element_type=F32
    )
    grad_key = jnp.einsum(
        "shqk,sqhe->skhe", grad_raw, split_heads(query_rows, DEC), preferred_element_type=F32
    )
    return (
        merge_heads(grad_query).astype(BF16),
        merge_heads(grad_key).astype(BF16),
        merge_heads(grad_value).astype(BF16),
    )


def masks_for(dec_lengths, mem_lengths):
    row_ids = jnp.arange(DEC)
    inside = row_ids[None, :] < dec_lengths[:, None]
    valid_rows = inside.reshape(-1, 1)
    causal = (row_ids[None, None, :] <= row_ids[None, :, None]) & inside[:, None, :]
    mem_seen = (jnp.arange(MEM)[None, :] < mem_lengths[:, None])[:, None, :]
    mem_seen = jnp.broadcast_to(mem_seen, (mem_lengths.shape[0], DEC, MEM))
    return (valid_rows, causal, mem_seen)


def run_forward(weights, hidden, mem_rows, dec_lengths, mem_lengths):
    (
        self_project,
        self_output,
        cross_query,
        cross_memory,
        cross_output,
        feed_in,
        feed_out,
        bias_rows,
        feed_bias,
        norm_gains,
        norm_shifts,
    ) = weights
    bias_full = bias_rows.astype(F32)
    gain_full = norm_gains.astype(F32)
    shift_full = norm_shifts.astype(F32)
    valid_rows, causal, mem_seen = masks_for(dec_lengths, mem_lengths)
    projected = product(hidden, self_project)
    query_rows = (projected[:, :D] + bias_full[0]).astype(BF16)
    key_rows = projected[:, D : 2 * D].astype(BF16)
    value_rows = (projected[:, 2 * D :] + bias_full[1]).astype(BF16)
    mixed, log_one = attend(query_rows, key_rows, value_rows, causal)
    resid_one = alpha_res * hidden.astype(F32) + product(mixed, self_output) + bias_full[2]
    first, scaled_one, inv_one = layer_norm(resid_one, gain_full[0], shift_full[0])
    first = first.astype(BF16)
    cross_q = (product(first, cross_query) + bias_full[3]).astype(BF16)
    mem_proj = product(mem_rows, cross_memory)
    cross_k = mem_proj[:, :D].astype(BF16)
    cross_v = (mem_proj[:, D:] + bias_full[4]).astype(BF16)
    mixed_two, log_two = attend(cross_q, cross_k, cross_v, mem_seen)
    resid_two = (
        alpha_res * first.astype(F32) + product(mixed_two, cross_output) + bias_full[5]
    )
    second, scaled_two, inv_two = layer_norm(resid_two, gain_full[1], shift_full[1])
    second = second.astype(BF16)
    pre_act = product(second, feed_in) + feed_bias.astype(F32)
    active = gelu_tanh(pre_act).astype(BF16)
    resid_three = alpha_res * second.astype(F32) + product(active, feed_out) + bias_full[6]
    normed, scaled_three, inv_three = layer_norm(resid_three, gain_full[2], shift_full[2])
    block_out = jnp.where(valid_rows, normed, 0.0).astype(BF16)
    saved = (
        query_rows,
        key_rows,
        value_rows,
        log_one,
        mixed,
        scaled_one,
        inv_one,
        first,
        cross_q,
        cross_k,
        cross_v,
        log_two,
        mixed_two,
        scaled_two,
        inv_two,
        second,
        pre_act,
        active,
        scaled_three,
        inv_three,
    )
    return (saved, block_out)


def run_backward(weights, saved, hidden, mem_rows, cot_rows, dec_lengths, mem_lengths):
    (
        self_project,
        self_output,
        cross_query,
        cross_memory,
        cross_output,
        feed_in,
        feed_out,
        bias_rows,
        feed_bias,
        norm_gains,
        norm_shifts,
    ) = weights
    (
        query_rows,
        key_rows,
        value_rows,
        log_one,
        mixed,
        scaled_one,
        inv_one,
        first,
        cross_q,
        cross_k,
        cross_v,
        log_two,
        mixed_two,
        scaled_two,
        inv_two,
        second,
        pre_act,
        active,
        scaled_three,
        inv_three,
    ) = saved
    gain_full = norm_gains.astype(F32)
    valid_rows, causal, mem_seen = masks_for(dec_lengths, mem_lengths)
    grad_top = jnp.where(valid_rows, cot_rows.astype(F32), 0.0)
    grad_three, gain_three, shift_three = norm_back(grad_top, scaled_three, inv_three, gain_full[2])
    branch_three = grad_three.astype(BF16)
    grad_feed_out = outer_sum(active, branch_three)
    grad_pre = (times_trans(branch_three, feed_out) * gelu_slope(pre_act)).astype(BF16)
    grad_feed_in = outer_sum(second, grad_pre)
    grad_second = (alpha_res * grad_three + times_trans(grad_pre, feed_in)).astype(BF16)
    grad_two, gain_two, shift_two = norm_back(
        grad_second.astype(F32), scaled_two, inv_two, gain_full[1]
    )
    branch_two = grad_two.astype(BF16)
    grad_cross_output = outer_sum(mixed_two, branch_two)
    grad_mixed_two = times_trans(branch_two, cross_output).astype(BF16)
    grad_cq, grad_ck, grad_cv = attend_back(
        cross_q, cross_k, cross_v, mem_seen, log_two, grad_mixed_two
    )
    grad_mem_proj = jnp.concatenate([grad_ck, grad_cv], 1)
    grad_cross_memory = outer_sum(mem_rows, grad_mem_proj)
    grad_mem_rows = times_trans(grad_mem_proj, cross_memory).astype(BF16)
    grad_cross_query = outer_sum(first, grad_cq)
    grad_first = (alpha_res * grad_two + times_trans(grad_cq, cross_query)).astype(BF16)
    grad_one, gain_one, shift_one = norm_back(
        grad_first.astype(F32), scaled_one, inv_one, gain_full[0]
    )
    branch_one = grad_one.astype(BF16)
    grad_self_output = outer_sum(mixed, branch_one)
    grad_mixed = times_trans(branch_one, self_output).astype(BF16)
    grad_q, grad_k, grad_v = attend_back(
        query_rows, key_rows, value_rows, causal, log_one, grad_mixed
    )
    grad_projected = jnp.concatenate([grad_q, grad_k, grad_v], 1)
    grad_self_project = outer_sum(hidden, grad_projected)
    grad_hidden = (alpha_res * grad_one + times_trans(grad_projected, self_project)).astype(
        BF16
    )
    grad_bias_rows = jnp.stack(
        [
            column_total(grad_q),
            column_total(grad_v),
            column_total(branch_one),
            column_total(grad_cq),
            column_total(grad_cv),
            column_total(branch_two),
            column_total(branch_three),
        ]
    )
    grads = (
        grad_self_project,
        grad_self_output,
        grad_cross_query,
        grad_cross_memory,
        grad_cross_output,
        grad_feed_in,
        grad_feed_out,
        grad_bias_rows,
        column_total(grad_pre),
        jnp.stack([gain_one, gain_two, gain_three]),
        jnp.stack([shift_one, shift_two, shift_three]),
    )
    return (grads, grad_hidden, grad_mem_rows)


SMALL = 13


def pack_small(bias_rows, feed_bias, norm_gains, norm_shifts):
    rows = jnp.concatenate([bias_rows, norm_gains, norm_shifts], 0)
    span = rows.shape[1]
    lane = lax.broadcasted_iota(jnp.int32, (SMALL, 128), 1) // span
    rows = jnp.where(lane == lax.axis_index("shard"), jnp.tile(rows, (1, 128 // span)), 0)
    rest = jnp.zeros((2, 128), BF16)
    return jnp.concatenate([rows, feed_bias[None], rest], 0)


def hand_out_kernel(count, *refs):
    small, large, refs = refs[0], refs[1 : 1 + count], refs[1 + count :]
    bias, feed, gains, shifts = refs[:4]
    outs, held, sem = refs[4 : 4 + count], refs[4 + count : 4 + 2 * count], refs[-1]
    reads = [pltpu.make_async_copy(large[k], held[k], sem.at[0, k]) for k in range(count)]
    writes = [pltpu.make_async_copy(held[k], outs[k], sem.at[1, k]) for k in range(count)]
    for copy in reads:
        copy.start()
    shard = lax.axis_index("shard")
    mine = jnp.zeros((16, 32), F32)
    for k in range(4):
        mine += jnp.where(shard == k, small[:, k * 32 : k * 32 + 32], 0.0)
    bias[...] = mine[:7]
    gains[...] = mine[7:10]
    shifts[...] = mine[10:SMALL]
    feed[...] = small[SMALL : SMALL + 1]
    for read, write in zip(reads, writes):
        read.wait()
        write.start()
    for copy in writes:
        copy.wait()


def hand_out(small, large):
    any_spec = pl.BlockSpec(memory_space=pl.ANY)
    vmem = pl.BlockSpec(memory_space=pltpu.VMEM)
    count = len(large)
    vectors = [jax.ShapeDtypeStruct(shape, F32) for shape in ((7, 32), (1, 128), (3, 32), (3, 32))]
    bias, feed, gains, shifts, *rest = pl.pallas_call(
        functools.partial(hand_out_kernel, count),
        out_shape=vectors + [jax.ShapeDtypeStruct(a.shape, a.dtype) for a in large],
        in_specs=[vmem] + [any_spec] * count,
        out_specs=[vmem] * 4 + [any_spec] * count,
        scratch_shapes=[pltpu.VMEM(a.shape, a.dtype) for a in large] + [pltpu.SemaphoreType.DMA((2, count))],
        compiler_params=pltpu.CompilerParams(vmem_limit_bytes=VMEM_LIMIT),
        name="hand_out",
    )(small, *large)
    return (*rest, bias, feed[0], gains, shifts)


def gather_by_collectives(owned):
    axis = [0] * 7 + [1, 0, 1, 1]
    return tuple(lax.all_gather(a, AXES, axis=d, tiled=True) for a, d in zip(owned, axis))


def scatter_by_collectives(grads, factor):
    axis = [0] * 7 + [1, 0, 1, 1]
    return tuple(
        lax.psum_scatter(a * factor, AXES, scatter_dimension=d, tiled=True) for a, d in zip(grads, axis)
    )


def body(by_kernel, hidden_in, memory, dec_lengths, mem_lengths, cotangent, *owned):
    token_count = hidden_in.shape[0] * lax.axis_size(AXES)
    factor = float(token_count) ** (-0.5)
    if by_kernel:
        packed = (pack_small(*owned[7:]), *owned[:7])
        block_out, grad_hidden, grad_memory, *shares = layer_call(
            hidden_in, memory, dec_lengths, mem_lengths, cotangent, packed, factor
        )
        return hand_out(shares[0], (block_out, grad_hidden, grad_memory, *shares[1:]))
    weights = gather_by_collectives(owned)
    saved, block_out = run_forward(weights, hidden_in, memory, dec_lengths, mem_lengths)
    grads, grad_hidden, grad_memory = run_backward(
        weights, saved, hidden_in, memory, cotangent, dec_lengths, mem_lengths
    )
    return (block_out, grad_hidden, grad_memory, *scatter_by_collectives(grads, factor))


def solution(mesh):
    rows, columns, vector = P(AXES, None), P(None, AXES), P(AXES)
    in_specs = (rows, rows, vector, vector, rows, *[rows] * 7, columns, vector, columns, columns)
    out_specs = (rows, rows, rows, *[rows] * 7, columns, vector, columns, columns)
    by_kernel = mesh.shape["dp"] == 8 and mesh.shape["shard"] == 4
    return jax.shard_map(
        functools.partial(body, by_kernel), mesh=mesh, in_specs=in_specs, out_specs=out_specs, check_vma=False
    )
```
